128 devices in a mesh: seq: 32 (over x, z, core), grp: 4 (over y).
Axes of the slice: x: 4, y: 4, z: 4, core: 2. Of those that a mesh axis runs over, the one named last changes fastest.
Arguments:
- candidates: bfloat16 [4, 32, 128, 1024], P('grp', 'seq'), may hold values from -27 to 27
- block_user: int32 [4, 32], P('grp'), may hold values from 0 to 3
- hist_len: int32 [4, 4], P('grp'), may hold values from 1 to 16384
- key_cache: bfloat16 [4, 4, 16384, 1024], P('grp', None, 'seq'), may hold values from -6 to 6
- value_cache: bfloat16 [4, 4, 16384, 1024], P('grp', None, 'seq'), may hold values from -6 to 6
- w_in: bfloat16 [1024, 2048], P(None, 'grp'), may hold values from -0.1875 to 0.1875
- w_out: bfloat16 [1024, 1024], P('grp'), may hold values from -0.1875 to 0.1875
Outputs:
- updated: bfloat16 [4, 32, 128, 1024], P('grp', 'seq')
The draws below stay inside these ranges and needn't reach their ends.
Inputs may be any that keep to these rules, and one draw needn't show every extreme that they name: `block_user`: each block's user is numbered within the block's own group. `hist_len`: a user's cached events occupy history positions 0 to its count minus one.
All inputs are finite; a program needn't handle non-finite values.
Results may differ from the reference program's by a relative error of at most 0.0049.
Values may be sent and summed in bfloat16 or wider, within the bound.
A program may use at most 192 MiB of HBM per device.

```python
import math
import jax
import jax.numpy as jnp
import numpy as np
from jax import lax

D = 1024
HEADS = 8
BLOCK = 128
USERS_GRP = 4
GROUPS = 4
GROUP_BLOCKS = 32
HIST = 16384


def draw_candidates(key, part):
    key = jax.random.fold_in(key, 11)
    key_base, key_rows, key_cols = jax.random.split(key, 3)
    shape = (GROUPS, GROUP_BLOCKS, BLOCK, D)
    base = jnp.clip(jax.random.normal(key_base, shape, jnp.float32), -6.0, 6.0)
    row_scale = jnp.exp(jax.random.uniform(key_rows, (GROUPS, GROUP_BLOCKS, BLOCK, 1), jnp.float32, math.log(0.3), math.log(3.0)))
    col_scale = jnp.exp(jax.random.uniform(key_cols, (1, 1, 1, D), jnp.float32, math.log(0.6), math.log(1.5)))
    return (base * row_scale * col_scale).astype(jnp.bfloat16)


def touch_ends(entries, rng, smallest, largest):
    longest = entries.shape.index(max(entries.shape))
    spots = []
    for shift in (0, 1):
        where = [jax.random.randint(jax.random.fold_in(rng, axis), (), 0, length) for axis, length in enumerate(entries.shape)]
        where[longest] = (where[longest] + shift) % entries.shape[longest]
        spots.append(tuple(where))
    return entries.at[spots[0]].set(smallest).at[spots[1]].set(largest)


def level_of(own_key, extent, cuts, low, largest):
    def one(axis_at, parts):
        draws = jax.random.uniform(jax.random.fold_in(jax.random.fold_in(own_key, 6), axis_at), (parts,), jnp.float32, low / len(cuts), largest / len(cuts))
        return jnp.repeat(jnp.exp(draws), extent[axis_at] // parts).reshape((-1,) + (1,) * (len(extent) - axis_at - 1))

    gain = one(*cuts[0])
    for cut in cuts[1:]:
        gain = gain * one(*cut)
    return gain


def rank_bounds(number_of, slope):
    loads = [(1 << 20) // math.isqrt(standing ** slope) + 1 for standing in range(1, number_of + 1)]
    spread = 1 + sum(loads) // (1 << 30)
    return np.cumsum(np.array([max(1, weight // spread) for weight in loads]))


def ranked(own_key, shape, number_of, skew):
    listing = rank_bounds(number_of, skew)
    lot = jax.random.randint(jax.random.fold_in(own_key, 1), shape, 0, int(listing[number_of - 1]))
    rank = jnp.searchsorted(jnp.asarray(listing, jnp.int32), lot, side="right")
    return jax.random.permutation(jax.random.fold_in(own_key, 2), number_of)[rank].astype(jnp.int32)


def gaussian(rng, shape, width, limit, cuts=(), kind=jnp.bfloat16):
    result = width * jax.random.normal(rng, shape, jnp.float32)
    if cuts:
        result = result * level_of(rng, shape, cuts, -0.22, 0.18)
    return jnp.clip(result, -limit, limit).astype(kind)


def setup_inputs(seed: int = 0) -> dict:
    keys = jax.random.split(jax.random.key(seed), 8)
    return {
        "candidates": draw_candidates(jax.random.fold_in(keys[7], 71), 0),
        "block_user": touch_ends(ranked(keys[1], (GROUPS, GROUP_BLOCKS), USERS_GRP, 2), jax.random.fold_in(keys[1], 3), 0, USERS_GRP - 1).astype(jnp.int32),
        "hist_len": touch_ends(jax.random.randint(keys[2], (GROUPS, USERS_GRP), 1, HIST + 1), jax.random.fold_in(keys[2], 1), 1, HIST).astype(jnp.int32),
        "key_cache": gaussian(keys[3], (GROUPS, USERS_GRP, HIST, D), 1.0, 6.0, ((0, 4), (2, 32))),
        "value_cache": gaussian(keys[4], (GROUPS, USERS_GRP, HIST, D), 1.0, 6.0, ((0, 4), (2, 32))),
        "w_in": gaussian(keys[5], (D, 2 * D), D ** -0.5, 0.1875, ((1, 4),)),
        "w_out": gaussian(keys[6], (D, D), D ** -0.5, 0.1875, ((0, 4),)),
    }


EPSILON = 1e-05

def layer_norm(values_in):
    row_mean = lax.optimization_barrier(jnp.mean(values_in, axis=-1, keepdims=True))
    centered = values_in - row_mean
    variance = lax.optimization_barrier(jnp.mean(centered * centered, axis=-1, keepdims=True))
    return centered * lax.rsqrt(variance + EPSILON)

def reference(candidates, block_user, hist_len, key_cache, value_cache, w_in, w_out):
    head_size = D // HEADS
    scale_factor = 1.0 / math.sqrt(head_size)
    residual_in = candidates.astype(jnp.float32)
    normed = layer_norm(residual_in).astype(jnp.bfloat16)
    flat_rows = normed.reshape(GROUPS * GROUP_BLOCKS * BLOCK, D)
    projected = jax.nn.silu(jnp.dot(flat_rows, w_in, preferred_element_type=jnp.float32)).astype(jnp.bfloat16)
    gate_part = projected[:, :D]
    queries = projected[:, D:].reshape(GROUPS * GROUP_BLOCKS, BLOCK, HEADS, head_size)
    group_ids = (jnp.arange(GROUPS * GROUP_BLOCKS, dtype=jnp.int32) // GROUP_BLOCKS).astype(jnp.int32)
    owners = block_user.reshape(GROUPS * GROUP_BLOCKS).astype(jnp.int32)
    positions = jnp.arange(HIST, dtype=jnp.int32)

    def per_block(block_item):
        query_part, group_id, owner = block_item
        chosen_keys = key_cache[group_id, owner].reshape(HIST, HEADS, head_size).astype(jnp.float32)
        chosen_values = value_cache[group_id, owner].reshape(HIST, HEADS, head_size).astype(jnp.float32)
        owner_length = hist_len[group_id, owner]
        scores = jnp.einsum('qhd,khd->hqk', query_part.astype(jnp.float32), chosen_keys) * scale_factor
        live_mask = positions[None, None, :] < owner_length
        attention = jnp.where(live_mask, jax.nn.silu(scores), jnp.float32(0.0)).astype(jnp.bfloat16)
        mixed = jnp.einsum('hqk,khd->qhd', attention.astype(jnp.float32), chosen_values)
        return mixed.reshape(BLOCK, D)
    attended = lax.map(per_block, (queries, group_ids, owners))
    gated = (layer_norm(attended.reshape(GROUPS * GROUP_BLOCKS * BLOCK, D)) * gate_part.astype(jnp.float32)).astype(jnp.bfloat16)
    updated = residual_in.reshape(GROUPS * GROUP_BLOCKS * BLOCK, D) + jnp.dot(gated, w_out, preferred_element_type=jnp.float32)
    return updated.astype(jnp.bfloat16).reshape(GROUPS, GROUP_BLOCKS, BLOCK, D)
```

```python
import math

import jax
import jax.numpy as jnp
from jax import lax
from jax.experimental import pallas as pl
from jax.experimental.pallas import tpu as pltpu
from jax.sharding import PartitionSpec as P

HEADS = 8
EPSILON = 1e-05


def layer_norm(values_in):
    row_mean = jnp.mean(values_in, axis=-1, keepdims=True)
    centered = values_in - row_mean
    variance = jnp.mean(centered * centered, axis=-1, keepdims=True)
    return centered * lax.rsqrt(variance + EPSILON)


def silu_of_scores(scores, half_scale):
    half = scores * half_scale
    return (half + half * jnp.tanh(half)).astype(jnp.bfloat16)


def attention_kernel(owner_ref, limit_ref, q_ref, k_ref, v_ref, out_ref, live_ref):
    users, span, width = k_ref.shape
    blocks = q_ref.shape[0]
    head = width // HEADS
    half_scale = 0.5 / math.sqrt(head)

    def mask_user(u, carry):
        rows = lax.broadcasted_iota(jnp.int32, (span, head), 0)
        keep = jnp.where(rows < limit_ref[u], 1.0, 0.0).astype(jnp.bfloat16)
        for h in range(HEADS):
            cols = slice(h * head, (h + 1) * head)
            live_ref[u, :, cols] = v_ref[u, :, cols] * keep
        return carry

    lax.fori_loop(0, users, mask_user, 0)

    def pair(t, carry):
        items = [(2 * t + b, h) for b in range(2) for h in range(HEADS)]

        def scores_of(i):
            j, h = items[i]
            cols = slice(h * head, (h + 1) * head)
            return lax.dot_general(
                k_ref[owner_ref[j], :, cols], q_ref[j, :, cols],
                (((1,), (1,)), ((), ())), preferred_element_type=jnp.float32,
            )

        pending = [scores_of(0), scores_of(1)]
        for i, (j, h) in enumerate(items):
            cols = slice(h * head, (h + 1) * head)
            if i + 2 < len(items):
                pending.append(scores_of(i + 2))
            weights = silu_of_scores(pending.pop(0), half_scale)
            out_ref[j, :, cols] = lax.dot_general(
                weights, live_ref[owner_ref[j], :, cols],
                (((0,), (0,)), ((), ())), preferred_element_type=jnp.float32,
            ).astype(out_ref.dtype)
        return carry

    lax.fori_loop(0, blocks // 2, pair, 0)


def per_device(candidates, block_user, hist_len, key_cache, value_cache, w_in, w_out):
    local_blocks, block_rows, width = candidates.shape[1:]
    row_count = local_blocks * block_rows
    residual_in = candidates.reshape(row_count, width).astype(jnp.float32)
    normed = layer_norm(residual_in).astype(jnp.bfloat16)
    projected = jax.nn.silu(
        jnp.dot(
            normed,
            lax.all_gather(w_in, "grp", axis=1, tiled=True),
            preferred_element_type=jnp.float32,
        )
    ).astype(jnp.bfloat16)
    gate_part = projected[:, :width]
    queries = projected[:, width:].reshape(local_blocks, block_rows, width)
    all_queries = lax.all_gather(queries, "seq", axis=0, tiled=True)
    users, span = key_cache.shape[1], key_cache.shape[2]
    limits = hist_len[0] - lax.axis_index("seq") * span
    vmem = pl.BlockSpec(memory_space=pltpu.VMEM)
    smem = pl.BlockSpec(memory_space=pltpu.SMEM)
    terms = pl.pallas_call(
        attention_kernel,
        out_shape=jax.ShapeDtypeStruct(all_queries.shape, jnp.bfloat16),
        in_specs=[smem, smem, vmem, vmem, vmem],
        out_specs=vmem,
        scratch_shapes=[pltpu.VMEM((users, span, width), jnp.bfloat16)],
        compiler_params=pltpu.CompilerParams(vmem_limit_bytes=56 << 20),
        name="history_terms",
    )(block_user[0], limits, all_queries, key_cache[0], value_cache[0])
    attended = lax.psum_scatter(terms, "seq", scatter_dimension=0, tiled=True)
    attended = attended.reshape(row_count, width).astype(jnp.float32)
    gated = (layer_norm(attended) * gate_part.astype(jnp.float32)).astype(jnp.bfloat16)
    branch = jnp.dot(
        gated, lax.all_gather(w_out, "grp", axis=0, tiled=True), preferred_element_type=jnp.float32
    )
    updated = (residual_in + branch).astype(jnp.bfloat16)
    return updated.reshape(candidates.shape)


def solution(mesh):
    in_specs = (
        P("grp", "seq", None, None),
        P("grp", None),
        P("grp", None),
        P("grp", None, "seq", None),
        P("grp", None, "seq", None),
        P(None, "grp"),
        P("grp", None),
    )
    out_specs = P("grp", "seq", None, None)
    return jax.shard_map(
        per_device, mesh=mesh, in_specs=in_specs, out_specs=out_specs, check_vma=False
    )
```

```python
import math

import jax
import jax.numpy as jnp
from jax import lax
from jax.experimental import pallas as pl
from jax.experimental.pallas import tpu as pltpu
from jax.sharding import PartitionSpec as P

HEADS = 8
EPSILON = 1e-05
SIDE = 4
ROWS = 128
HALF = 64
QUARTER = 32
WIDTH = 1024
HEAD = WIDTH // HEADS
UNITS = SIDE * SIDE
CHUNKS = 4
LAG = 2

ORDER = [
    (1, 1), (1, 3), (3, 1), (3, 3),
    (2, 2), (2, 1), (1, 2), (2, 3),
    (3, 2), (2, 0), (0, 2), (1, 0),
    (3, 0), (0, 1), (0, 3), (0, 0),
]
PLACE = {offset: t for t, offset in enumerate(ORDER)}
CODE_X = sum(dx * 4**t for t, (dx, _) in enumerate(ORDER))
CODE_Z = sum(dz * 4**t for t, (_, dz) in enumerate(ORDER))


def normalize(values):
    mean = jnp.mean(values, axis=-1, keepdims=True)
    centered = values - mean
    variance = jnp.mean(centered * centered, axis=-1, keepdims=True)
    return centered * lax.rsqrt(variance + EPSILON)


def silu_of(values, half_scale):
    half = values * half_scale
    return half + half * jnp.tanh(half)


def place_of(a, along, across):
    return PLACE[(along % 4, across) if a == 0 else (across, along % 4)]


def schedule():
    ready = {t: t + 2 for t in range(UNITS)}
    events = [(ready[t], 0, "sum", (t,)) for t in range(UNITS)]
    done = {}
    for a in (0, 1):
        for d in range(4):
            steps = []
            for dirn, e in ((1, 1), (-1, 3)):
                step = max(ready[place_of(a, e, d)], ready[place_of(a, 2, d)] + LAG)
                events.append((step, 1, "dep", (a, dirn, 1 + d)))
                steps.append(step + LAG)
            done[a, d] = max([ready[place_of(a, 0, d)]] + steps)
            events.append((done[a, d], 2, "fin", (a, 1 + d)))
    for a in (0, 1):
        b = 1 - a
        steps = []
        for dirn, e in ((1, 1), (-1, 3)):
            step = max(done[b, e], done[b, 2] + LAG)
            events.append((step, 3, "dep", (a, dirn, 0)))
            steps.append(step + LAG)
        events.append((max([done[b, 0]] + steps), 4, "fin", (a, 0)))
    return sorted(events)


def layer_kernel(
    owner_ref, length_ref, cand_ref, k_hbm, v_hbm, win_hbm, wout_hbm, out_ref,
    keys, values, w_in, w_out, normed, stage, q_own, q_sib, part, sib, send, far, near,
    line, line_send, att, gate,
    local_sem, ag_send, ag_recv, w_send, w_recv, q_sems, p_send, p_recv, rs_send, rs_recv,
):
    seq = lax.axis_index("seq")
    y = lax.axis_index("grp")
    core = seq % 2
    z = (seq // 2) % 4
    x = seq // 8
    span = keys.shape[1]
    users = keys.shape[0]

    def at_chip(dx, dz):
        return (((x + dx) % 4) * 4 + (z + dz) % 4) * 2 + core

    neighbour = {
        (0, 1): at_chip(1, 0), (0, -1): at_chip(3, 0), (1, 1): at_chip(0, 1), (1, -1): at_chip(0, 3),
    }
    sibling = {"seq": seq - core + (1 - core)}
    outer_y = 3 - y
    inner_y = y + 1 - 2 * (y % 2)
    rest_y = 3 - inner_y

    def remote(src, dst, send_sem, recv_sem, device):
        return pltpu.make_async_remote_copy(
            src_ref=src, dst_ref=dst, send_sem=send_sem, recv_sem=recv_sem,
            device_id=device, device_id_type=pl.DeviceIdType.MESH,
        )

    barrier = pltpu.get_barrier_semaphore()
    peers = [{"seq": n} for n in neighbour.values()] + [sibling, {"grp": outer_y}, {"grp": inner_y}]
    for peer in peers:
        pl.semaphore_signal(barrier, inc=1, device_id=peer, device_id_type=pl.DeviceIdType.MESH)
    copies = [
        pltpu.make_async_copy(v_hbm, values, local_sem.at[0]),
        pltpu.make_async_copy(k_hbm, keys, local_sem.at[1]),
        pltpu.make_async_copy(win_hbm, w_in.at[y], local_sem.at[2]),
        pltpu.make_async_copy(wout_hbm, w_out.at[y], local_sem.at[3]),
    ]
    for copy in copies:
        copy.start()

    own_slot = x * 4 + z
    normed[own_slot] = normalize(cand_ref[...].astype(jnp.float32)).astype(jnp.bfloat16)
    pl.semaphore_wait(barrier, len(peers))

    in_half = w_in.shape[1] // 2
    in_rows = in_half // CHUNKS
    out_half = w_out.shape[1] // 2

    def weight(which, chunk, receiving=False):
        array, hbm = (w_in, win_hbm) if chunk < CHUNKS else (w_out, wout_hbm)
        half, rows = (in_half, in_rows) if chunk < CHUNKS else (out_half, out_half)
        first = (0 if chunk == CHUNKS else chunk * rows)
        side = core
        if which < 3:
            shard = {0: y, 1: y, 2: outer_y}[which]
            if receiving:
                shard = {0: outer_y, 1: inner_y, 2: rest_y}[which]
            device = {"grp": outer_y if which == 0 else inner_y}
        else:
            shard = {3: outer_y, 4: inner_y, 5: rest_y}[which]
            device = sibling
            if receiving:
                side = 1 - core
        rows_at = pl.ds(pl.multiple_of(side * half + first, 16), rows)
        src = array.at[shard, rows_at, :]
        if which < 2 and not receiving:
            src = hbm.at[rows_at, :]
        i = which * (CHUNKS + 1) + chunk
        return remote(src, array.at[shard, rows_at, :], w_send.at[i], w_recv.at[i], device)

    def start_own(which, chunks):
        for chunk in chunks:
            weight(which, chunk).start()

    def take(which, chunks):
        for chunk in chunks:
            weight(which, chunk, True).wait_recv()
            if which == 0:
                weight(2, chunk).start()
            weight({0: 3, 1: 4, 2: 5}[which], chunk).start()

    def take_sibling(which, chunks):
        for chunk in chunks:
            weight(which, chunk, True).wait_recv()

    in_chunks = range(CHUNKS)
    out_chunks = [CHUNKS]

    def ag(a, dirn, idx, is_far, receiving=False):
        half = 0 if (a == 0) == (idx == 0) else 1
        d = max(idx - 1, 0)
        along = (-dirn if is_far else 0) - (dirn if receiving else 0)
        dx, dz = (along, d) if a == 0 else (d, along)
        slot = ((x + dx % 4) % 4) * 4 + (z + dz % 4) % 4
        first, count = half * HALF, HALF
        if is_far:
            first, count = first + (0 if dirn > 0 else QUARTER), QUARTER
        ref = normed.at[slot, pl.ds(first, count), :]
        i = ((a * 2 + (dirn + 1) // 2) * 5 + idx) * 2 + int(is_far)
        return remote(ref, ref, ag_send.at[i], ag_recv.at[i], {"seq": neighbour[a, dirn]})

    ways = [(a, dirn) for a in (0, 1) for dirn in (1, -1)]

    def ag_start(idxs, is_far):
        for idx in idxs:
            for a, dirn in ways:
                ag(a, dirn, idx, is_far).start()

    def ag_take(idxs, is_far):
        for idx in idxs:
            for a, dirn in ways:
                ag(a, dirn, idx, is_far, True).wait_recv()

    def ag_1():
        ag_take([0], False)
        ag_start([0], True)
        ag_start([2, 4], False)

    def ag_2():
        ag_take([1], False)
        ag_start([1], True)

    def ag_3():
        ag_take([0], True)
        ag_start([3], False)

    def ag_4():
        ag_take([2, 4], False)
        ag_start([2, 4], True)

    def ag_5():
        ag_take([1], True)

    def ag_6():
        ag_take([3], False)
        ag_start([3], True)

    def ag_7():
        ag_take([2, 4], True)
        ag_take([3], True)

    ag_start([0, 1], False)
    start_own(0, in_chunks)

    @pl.when(y >= 2)
    def _():
        start_own(1, in_chunks)

    for copy in copies:
        copy.wait()
    offset = seq * span

    def mask_user(u, carry):
        rows = lax.broadcasted_iota(jnp.int32, (span, HEAD), 0)
        keep = jnp.where(rows < length_ref[u] - offset, 1.0, 0.0).astype(jnp.bfloat16)
        for h in range(HEADS):
            cols = slice(h * HEAD, (h + 1) * HEAD)
            values[u, :, cols] = values[u, :, cols] * keep
        return carry

    lax.fori_loop(0, users, mask_user, 0)

    ag_1()

    def early(chunks):
        @pl.when(y < 2)
        def _():
            take(0, chunks)

        @pl.when(y >= 2)
        def _():
            take(1, chunks)

    early([0, 1])
    ag_2()
    ag_3()
    early([2, 3])
    ag_4()

    @pl.when(y < 2)
    def _():
        take(2, in_chunks)
        take_sibling(3, in_chunks)
        take_sibling(5, in_chunks)

    @pl.when(y >= 2)
    def _():
        take_sibling(4, in_chunks)

    def late_1():
        @pl.when(y < 2)
        def _():
            start_own(1, in_chunks)

        @pl.when(y >= 2)
        def _():
            take(0, in_chunks)

    def late_2():
        @pl.when(y < 2)
        def _():
            take(1, in_chunks)

        @pl.when(y >= 2)
        def _():
            take(2, in_chunks)

        start_own(0, out_chunks)
        start_own(1, out_chunks)

    def late_3():
        take(0, out_chunks)
        take(1, out_chunks)

    def late_4():
        take(2, out_chunks)
        for which in (3, 4, 5):
            take_sibling(which, out_chunks)

        @pl.when(y < 2)
        def _():
            take_sibling(4, in_chunks)

        @pl.when(y >= 2)
        def _():
            take_sibling(3, in_chunks)
            take_sibling(5, in_chunks)

    def make_gate():
        own = normed[own_slot]
        for shard in (0, 1):
            got = jnp.dot(own, w_in[shard], preferred_element_type=jnp.float32)
            gate[:, shard * 512 : (shard + 1) * 512] = silu_of(got, 0.5).astype(jnp.bfloat16)

    def rs_half(a, idx):
        return 1 - a if idx > 0 else a

    def rs_source(a, idx, e):
        half = rs_half(a, idx)
        if idx > 0:
            t = place_of(a, e, idx - 1)
            return send.at[t, pl.ds(half * HALF, HALF), :], part.at[t, pl.ds(half * HALF, HALF), :]
        return line_send.at[half, e], line.at[half, e]

    def rs(a, dirn, idx, kind):
        e = 2 if kind == 0 else (1 if dirn > 0 else 3)
        first = 0 if (kind != 1) == (dirn > 0) else QUARTER
        w = (a * 2 + (dirn + 1) // 2) * 5 + idx
        src = rs_source(a, idx, e)[0].at[pl.ds(first, QUARTER), :]
        dst = far.at[w] if kind == 0 else near.at[w, pl.ds(first, QUARTER), :]
        return remote(
            src, dst, rs_send.at[w * 3 + kind], rs_recv.at[w * 3 + kind], {"seq": neighbour[a, dirn]}
        )

    def rs_first_sends(a, idx, e):
        if e == 2:
            rs(a, 1, idx, 0).start()
            rs(a, -1, idx, 0).start()
        elif e != 0:
            rs(a, 1 if e == 1 else -1, idx, 1).start()

    def partial_copy(t):
        rows = pl.ds(pl.multiple_of(t * ROWS, ROWS), ROWS)
        return remote(q_sib.at[rows, :], sib.at[t], p_send.at[t], p_recv.at[t], sibling)

    def do_sum(t):
        partial_copy(t).wait_recv()
        total = part[t] + sib[t].astype(jnp.float32)
        part[t] = total
        send[t] = total.astype(jnp.bfloat16)
        dx, dz = ORDER[t]
        rs_first_sends(1, 1 + dx, dz)
        rs_first_sends(0, 1 + dz, dx)

    def do_dep(a, dirn, idx):
        rs(a, dirn, idx, 0).wait_recv()
        e, first = (1, 0) if dirn > 0 else (3, QUARTER)
        w = (a * 2 + (dirn + 1) // 2) * 5 + idx
        to_send, exact = rs_source(a, idx, e)
        rows = pl.ds(first, QUARTER)
        to_send[rows, :] = (exact[rows, :] + far[w].astype(jnp.float32)).astype(jnp.bfloat16)
        rs(a, dirn, idx, 2).start()

    def do_fin(a, idx):
        for dirn in (1, -1):
            for kind in (1, 2):
                rs(a, dirn, idx, kind).wait_recv()
        up, down = a * 10 + 5 + idx, a * 10 + idx
        total = rs_source(a, idx, 0)[1][...] + near[up].astype(jnp.float32) + near[down].astype(jnp.float32)
        half = rs_half(a, idx)
        if idx == 0:
            att[half * HALF : (half + 1) * HALF, :] = total
        else:
            line[half, idx - 1] = total
            line_send[half, idx - 1] = total.astype(jnp.bfloat16)
            rs_first_sends(1 - a, 0, idx - 1)

    steps = {}
    for step, _, kind, args in schedule():
        steps.setdefault(step, []).append((kind, args))

    def run_step(step):
        for kind, args in steps.get(step, []):
            {"sum": do_sum, "dep": do_dep, "fin": do_fin}[kind](*args)

    def queries_copy(b):
        rows = pl.ds(pl.multiple_of(b * 4 * ROWS, ROWS), 4 * ROWS)
        return remote(q_own.at[rows, :], q_sib.at[rows, :], q_sems.at[b], q_sems.at[4 + b], sibling)

    def project(b, code_x, code_z):
        for m in range(4):
            dx, dz = (code_x // 4**m) % 4, (code_z // 4**m) % 4
            slot = ((x + dx) % 4) * 4 + (z + dz) % 4
            stage[m * ROWS : (m + 1) * ROWS, :] = normed[slot]

        def columns(i, carry):
            got = jnp.dot(
                stage[...], w_in[2 + i // 2, :, pl.ds(pl.multiple_of((i % 2) * 256, 256), 256)],
                preferred_element_type=jnp.float32,
            )
            rows = pl.ds(pl.multiple_of(b * 4 * ROWS, ROWS), 4 * ROWS)
            q_own[rows, pl.ds(pl.multiple_of(i * 256, 256), 256)] = silu_of(got, 0.5).astype(jnp.bfloat16)
            return carry

        lax.fori_loop(0, 4, columns, 0)
        queries_copy(b).start()

    half_scale = 0.5 / math.sqrt(HEAD)

    def unit(t, dx, dz):
        chip = ((x + dx) % 4) * 4 + (z + dz) % 4
        rows = pl.ds(pl.multiple_of(t * ROWS, ROWS), ROWS)
        owners = [owner_ref[2 * chip + core], owner_ref[2 * chip + 1 - core]]
        items = [(b, h) for b in range(2) for h in range(HEADS)]

        def scores_of(i):
            b, h = items[i]
            cols = slice(h * HEAD, (h + 1) * HEAD)
            queries = (q_own, q_sib)[b][rows, cols]
            return lax.dot_general(
                keys[owners[b], :, cols], queries,
                (((1,), (1,)), ((), ())), preferred_element_type=jnp.float32,
            )

        pending = [scores_of(0), scores_of(1)]
        for i, (b, h) in enumerate(items):
            cols = slice(h * HEAD, (h + 1) * HEAD)
            if i + 2 < len(items):
                pending.append(scores_of(i + 2))
            weights = silu_of(pending.pop(0), half_scale).astype(jnp.bfloat16)
            got = lax.dot_general(
                weights, values[owners[b], :, cols],
                (((0,), (0,)), ((), ())), preferred_element_type=jnp.float32,
            )
            if b == 0:
                part[t, :, cols] = got
            else:
                q_sib[rows, cols] = got.astype(jnp.bfloat16)

    extras = {0: [ag_5], 1: [ag_6], 3: [late_1], 6: [late_2], 9: [late_3], 12: [late_4], 14: [make_gate]}

    def step_body(s, carry):
        proj_x, proj_z, unit_x, unit_z = carry

        @pl.when(s == 4)
        def _():
            ag_7()

        @pl.when((s % 4 == 0) & (s < UNITS))
        def _():
            project(s // 4, proj_x, proj_z)

        @pl.when(s >= 1)
        def _():
            t = s - 1

            @pl.when(t % 4 == 0)
            def _():
                queries_copy(t // 4).wait_recv()

            unit(t, unit_x % 4, unit_z % 4)
            partial_copy(t).start()

        for k in range(UNITS + 1):
            todo = extras.get(k, [])
            if todo or k in steps:

                @pl.when(s == k)
                def _(k=k, todo=todo):
                    for action in todo:
                        action()
                    run_step(k)

        at_batch = (s % 4) // 3
        proj_div = 1 + 255 * at_batch
        unit_div = 1 + 3 * ((s + UNITS) // (UNITS + 1))
        return proj_x // proj_div, proj_z // proj_div, unit_x // unit_div, unit_z // unit_div

    lax.fori_loop(0, UNITS + 1, step_body, (CODE_X, CODE_Z, CODE_X, CODE_Z))
    for step in sorted(steps):
        if step > UNITS:
            run_step(step)

    gated = (normalize(att[...]) * gate[...].astype(jnp.float32)).astype(jnp.bfloat16)
    branch = jnp.dot(
        gated, w_out[...].reshape(WIDTH, WIDTH), preferred_element_type=jnp.float32
    )
    out_ref[...] = (cand_ref[...].astype(jnp.float32) + branch).astype(jnp.bfloat16)

    for idx in range(5):
        for a, dirn in ways:
            for is_far in (False, True):
                ag(a, dirn, idx, is_far).wait_send()
            for kind in range(3):
                rs(a, dirn, idx, kind).wait_send()
    for which in range(6):
        for chunk in range(CHUNKS + 1):
            weight(which, chunk).wait_send()
    for b in range(4):
        queries_copy(b).wait_send()
    for t in range(UNITS):
        partial_copy(t).wait_send()


def per_device(candidates, block_user, hist_len, key_cache, value_cache, w_in, w_out):
    users, span, width = key_cache.shape[1:]
    vmem = pl.BlockSpec(memory_space=pltpu.VMEM)
    smem = pl.BlockSpec(memory_space=pltpu.SMEM)
    anywhere = pl.BlockSpec(memory_space=pl.ANY)
    bf16, f32 = jnp.bfloat16, jnp.float32
    dma = pltpu.SemaphoreType.DMA
    updated = pl.pallas_call(
        layer_kernel,
        out_shape=jax.ShapeDtypeStruct((ROWS, width), bf16),
        in_specs=[smem, smem, vmem, anywhere, anywhere, anywhere, anywhere],
        out_specs=vmem,
        scratch_shapes=[
            pltpu.VMEM((users, span, width), bf16),
            pltpu.VMEM((users, span, width), bf16),
            pltpu.VMEM((4,) + w_in.shape, bf16),
            pltpu.VMEM((4,) + w_out.shape, bf16),
            pltpu.VMEM((UNITS, ROWS, width), bf16),
            pltpu.VMEM((4 * ROWS, width), bf16),
            pltpu.VMEM((UNITS * ROWS, width), bf16),
            pltpu.VMEM((UNITS * ROWS, width), bf16),
            pltpu.VMEM((UNITS, ROWS, width), f32),
            pltpu.VMEM((UNITS, ROWS, width), bf16),
            pltpu.VMEM((UNITS, ROWS, width), bf16),
            pltpu.VMEM((20, QUARTER, width), bf16),
            pltpu.VMEM((20, HALF, width), bf16),
            pltpu.VMEM((2, 4, HALF, width), f32),
            pltpu.VMEM((2, 4, HALF, width), bf16),
            pltpu.VMEM((ROWS, width), f32),
            pltpu.VMEM((ROWS, width), bf16),
            dma((4,)),
            dma((40,)),
            dma((40,)),
            dma((6 * (CHUNKS + 1),)),
            dma((6 * (CHUNKS + 1),)),
            dma((8,)),
            dma((UNITS,)),
            dma((UNITS,)),
            dma((60,)),
            dma((60,)),
        ],
        compiler_params=pltpu.CompilerParams(
            collective_id=0, has_side_effects=True, vmem_limit_bytes=60 << 20
        ),
        name="layer",
    )(
        block_user[0], hist_len[0], candidates[0, 0], key_cache[0], value_cache[0], w_in, w_out
    )
    return updated.reshape(candidates.shape)


def solution(mesh):
    in_specs = (
        P("grp", "seq", None, None),
        P("grp", None),
        P("grp", None),
        P("grp", None, "seq", None),
        P("grp", None, "seq", None),
        P(None, "grp"),
        P("grp", None),
    )
    out_specs = P("grp", "seq", None, None)
    return jax.shard_map(
        per_device, mesh=mesh, in_specs=in_specs, out_specs=out_specs, check_vma=False
    )
```

```python
import math

import jax
import jax.numpy as jnp
from jax import lax
from jax.experimental import pallas as pl
from jax.experimental.pallas import tpu as pltpu
from jax.sharding import PartitionSpec as P

HEADS = 8
EPSILON = 1e-05
SIDE = 4
ROWS = 128
HALF = 64
QUARTER = 32
WIDTH = 1024
HEAD = WIDTH // HEADS
UNITS = SIDE * SIDE
ROW_CHUNKS = 4
CHUNKS = 2 * ROW_CHUNKS
STEPS = 16
LAG = 2

ORDER = [
    (0, 0), (1, 0), (3, 0), (0, 3),
    (1, 1), (3, 3), (1, 3), (0, 1),
    (2, 2), (2, 1), (1, 2), (2, 3),
    (3, 2), (2, 0), (0, 2), (3, 1),
]
PLACE = {offset: t for t, offset in enumerate(ORDER)}
CODES_X = [sum(dx * 4**t for t, (dx, _) in enumerate(ORDER[i : i + 8])) for i in (0, 8)]
CODES_Z = [sum(dz * 4**t for t, (_, dz) in enumerate(ORDER[i : i + 8])) for i in (0, 8)]
PARTS = [(0, 0), (1, 0), (1, 1), (2, 0), (2, 1), (3, 0), (3, 1), (0, 1)]
CODE = sum((batch + 4 * group) * 8**i for i, (batch, group) in enumerate(PARTS))


def shifted(code, base, when):
    return code + when * (lax.div(code, base) - code)


def digits(codes, batch):
    high = lax.div(batch, 2)
    return shifted(codes[0] + high * (codes[1] - codes[0]), 256, lax.rem(batch, 2))


def normalize(values):
    mean = jnp.mean(values, axis=-1, keepdims=True)
    centered = values - mean
    variance = jnp.mean(centered * centered, axis=-1, keepdims=True)
    return centered * lax.rsqrt(variance + EPSILON)


def silu_of(values, half_scale):
    half = values * half_scale
    return half + half * jnp.tanh(half)


def place_of(a, along, across):
    return PLACE[(along % 4, across) if a == 0 else (across, along % 4)]


def schedule():
    ready = {}
    for it in range(STEPS):
        batch, group = PARTS[it // 2]
        for n in range(2 * group):
            ready[0, 4 * batch + it % 2 * 2 + n] = it + 2
    events = [(step, 0, g, "sum", (t,)) for (g, t), step in ready.items()]
    for g in range(1):
        done = {}
        for a in (0, 1):
            for d in range(4):
                steps = []
                for dirn, e in ((1, 1), (-1, 3)):
                    step = max(ready[g, place_of(a, e, d)], ready[g, place_of(a, 2, d)] + LAG)
                    events.append((step, 1, g, "dep", (a, dirn, 1 + d)))
                    steps.append(step + LAG)
                done[a, d] = max([ready[g, place_of(a, 0, d)]] + steps)
                events.append((done[a, d], 2, g, "fin", (a, 1 + d)))
        for a in (0, 1):
            b = 1 - a
            steps = []
            for dirn, e in ((1, 1), (-1, 3)):
                step = max(done[b, e], done[b, 2] + LAG)
                events.append((step, 3, g, "dep", (a, dirn, 0)))
                steps.append(step + LAG)
            events.append((max([done[b, 0]] + steps), 4, g, "fin", (a, 0)))
    return sorted(events)


def layer_kernel(
    owner_ref, length_ref, cand_ref, k_hbm, v_hbm, win_hbm, wout_hbm, out_ref,
    keys, values, w_in, w_out, normed, stage, q_own, q_sib, part, part_sib, sib, send, far, near,
    line, line_send, att, gate,
    local_sem, ag_send, ag_recv, w_send, w_recv, q_sems, p_send, p_recv, rs_send, rs_recv,
):
    seq = lax.axis_index("seq")
    y = lax.axis_index("grp")
    core = lax.rem(seq, 2)
    z = lax.rem(lax.div(seq, 2), 4)
    x = lax.div(seq, 8)
    span = keys.shape[1]
    users = keys.shape[0]

    def at_chip(dx, dz):
        return (lax.rem(x + dx, 4) * 4 + lax.rem(z + dz, 4)) * 2 + core

    neighbour = {
        (0, 1): at_chip(1, 0), (0, -1): at_chip(3, 0), (1, 1): at_chip(0, 1), (1, -1): at_chip(0, 3),
    }
    sibling = {"seq": seq - core + (1 - core)}
    outer_y = 3 - y
    inner_y = y + 1 - 2 * lax.rem(y, 2)
    rest_y = 3 - inner_y

    def remote(src, dst, send_sem, recv_sem, device):
        return pltpu.make_async_remote_copy(
            src_ref=src, dst_ref=dst, send_sem=send_sem, recv_sem=recv_sem,
            device_id=device, device_id_type=pl.DeviceIdType.MESH,
        )

    barrier = pltpu.get_barrier_semaphore()
    peers = [{"seq": n} for n in neighbour.values()] + [sibling, {"grp": outer_y}, {"grp": inner_y}]
    for peer in peers:
        pl.semaphore_signal(barrier, inc=1, device_id=peer, device_id_type=pl.DeviceIdType.MESH)
    copies = [
        pltpu.make_async_copy(v_hbm, values, local_sem.at[0]),
        pltpu.make_async_copy(k_hbm, keys, local_sem.at[1]),
        pltpu.make_async_copy(win_hbm, w_in.at[y], local_sem.at[2]),
        pltpu.make_async_copy(wout_hbm, w_out.at[y], local_sem.at[3]),
    ]
    own_slot = x * 4 + z

    def by_rows(count, action):
        action(pl.ds(0, count))

    def norm_rows(rows):
        normed[own_slot, rows, :] = normalize(cand_ref[rows, :].astype(jnp.float32)).astype(jnp.bfloat16)

    by_rows(ROWS, norm_rows)
    pl.semaphore_wait(barrier, len(peers))

    in_half = w_in.shape[1] // 2
    in_rows = in_half // ROW_CHUNKS
    out_half = w_out.shape[1] // 2

    def weight(which, chunk, receiving=False):
        is_in = not (isinstance(chunk, int) and chunk == CHUNKS)
        array, hbm = (w_in, win_hbm) if is_in else (w_out, wout_hbm)
        half, rows = (in_half, in_rows) if is_in else (out_half, out_half)
        first = lax.rem(chunk, ROW_CHUNKS) * rows if is_in else 0
        cols = pl.ds(pl.multiple_of(lax.div(chunk, ROW_CHUNKS) * 256, 256), 256) if is_in else pl.ds(0, WIDTH)
        side = core
        if which < 3:
            to = (outer_y, inner_y, inner_y if is_in else outer_y)[which]
            shard = (y, y, outer_y if is_in else inner_y)[which]
            if receiving:
                shard = (outer_y, inner_y, rest_y)[which]
            device = {"grp": to}
        else:
            shard = (outer_y, inner_y, rest_y)[which - 3]
            device = sibling
            if receiving:
                side = 1 - core
        rows_at = pl.ds(pl.multiple_of(side * half + first, 16), rows)
        dst = array.at[shard, rows_at, cols]
        src = hbm.at[rows_at, cols] if which < 2 and not receiving else dst
        i = which * (CHUNKS + 1) + chunk
        return remote(src, dst, w_send.at[i], w_recv.at[i], device)

    def each(chunks, action):
        if len(chunks) == 1:
            action(chunks[0])
            return

        def some(chunk, carry):
            action(chunk)
            return carry

        lax.fori_loop(chunks[0], chunks[-1] + 1, some, 0)

    def start_own(which, chunks):
        each(chunks, lambda chunk: weight(which, chunk).start())

    def take(which, chunks):
        def one(chunk):
            weight(which, chunk, True).wait_recv()
            if which == (1 if chunks is out_chunks else 0):
                weight(2, chunk).start()
            weight(which + 3, chunk).start()

        each(chunks, one)

    def take_sibling(which, chunks):
        each(chunks, lambda chunk: weight(which, chunk, True).wait_recv())

    in_chunks = range(CHUNKS)
    out_chunks = [CHUNKS]

    def ag(a, dirn, idx, is_far, receiving=False):
        half = 0 if (a == 0) == (idx == 0) else 1
        d = max(idx - 1, 0)
        along = (-dirn if is_far else 0) - (dirn if receiving else 0)
        dx, dz = (along, d) if a == 0 else (d, along)
        slot = lax.rem(x + dx % 4, 4) * 4 + lax.rem(z + dz % 4, 4)
        first, count = half * HALF, HALF
        if is_far:
            first, count = first + (0 if dirn > 0 else QUARTER), QUARTER
        ref = normed.at[slot, pl.ds(first, count), :]
        i = ((a * 2 + (dirn + 1) // 2) * 5 + idx) * 2 + int(is_far)
        return remote(ref, ref, ag_send.at[i], ag_recv.at[i], {"seq": neighbour[a, dirn]})

    def ag_any(ref, i, device):
        return remote(ref, ref, ag_send.at[i], ag_recv.at[i], device)

    ways = [(a, dirn) for a in (0, 1) for dirn in (1, -1)]

    def ag_start(idxs, is_far):
        for idx in idxs:
            for a, dirn in ways:
                ag(a, dirn, idx, is_far).start()

    def ag_take(idxs, is_far):
        for idx in idxs:
            for a, dirn in ways:
                ag(a, dirn, idx, is_far, True).wait_recv()

    def ag_1():
        ag_take([0], False)
        ag_start([0], True)
        ag_start([2, 4], False)

    def ag_2():
        ag_take([1], False)
        ag_start([1], True)

    def ag_3():
        ag_take([0], True)
        ag_start([3], False)

    def ag_4():
        ag_take([2, 4], False)
        ag_start([2, 4], True)

    def ag_5():
        ag_take([1], True)

    def ag_6():
        ag_take([3], False)
        ag_start([3], True)

    def ag_7():
        ag_take([2, 4], True)
        ag_take([3], True)

    @pl.when(y >= 2)
    def _():
        def both(chunk):
            weight(0, chunk).start()
            weight(1, chunk).start()

        each(in_chunks, both)

    ag_start([0, 1], False)

    @pl.when(y < 2)
    def _():
        start_own(0, in_chunks)

    for copy in copies:
        copy.start()
    for copy in copies:
        copy.wait()
    offset = seq * span

    def mask_user(u, carry):
        rows = lax.broadcasted_iota(jnp.int32, (span, HEAD), 0)
        keep = jnp.where(rows < length_ref[u] - offset, 1.0, 0.0).astype(jnp.bfloat16)
        for h in range(HEADS):
            cols = slice(h * HEAD, (h + 1) * HEAD)
            values[u, :, cols] = values[u, :, cols] * keep
        return carry

    lax.fori_loop(0, users, mask_user, 0)

    def early(chunks):
        @pl.when(y < 2)
        def _():
            take(0, chunks)

        @pl.when(y >= 2)
        def _():
            take(1, chunks)

    def early_rest(chunks):
        @pl.when(y < 2)
        def _():
            take(2, chunks)
            take_sibling(3, chunks)
            take_sibling(5, chunks)

        @pl.when(y >= 2)
        def _():
            take_sibling(4, chunks)

    early([0, 1])
    ag_1()
    early([2, 3])
    ag_2()
    early_rest([0, 1, 2, 3])

    def late_1():
        @pl.when(y < 2)
        def _():
            start_own(1, in_chunks)

        @pl.when(y >= 2)
        def _():
            take(0, in_chunks)

        start_own(0, out_chunks)
        start_own(1, out_chunks)

    def late_2():
        @pl.when(y < 2)
        def _():
            take(1, in_chunks)

        @pl.when(y >= 2)
        def _():
            take(2, in_chunks)

    def late_3():
        take(1, out_chunks)
        take(0, out_chunks)

    def late_4():
        take(2, out_chunks)
        for which in (3, 4, 5):
            take_sibling(which, out_chunks)

        @pl.when(y < 2)
        def _():
            take_sibling(4, in_chunks)

        @pl.when(y >= 2)
        def _():
            take_sibling(3, in_chunks)
            take_sibling(5, in_chunks)

    def make_gate():
        own = normed[own_slot]
        for shard in (0, 1):
            got = jnp.dot(own, w_in[shard], preferred_element_type=jnp.float32)
            gate[:, shard * 512 : (shard + 1) * 512] = silu_of(got, 0.5).astype(jnp.bfloat16)

    def rs_half(a, idx):
        return 1 - a if idx > 0 else a

    def rs_source(g, a, idx, e):
        half = rs_half(a, idx)
        if idx > 0:
            t = place_of(a, e, idx - 1)
            rows = pl.ds(half * HALF, HALF)
            return send.at[g, t, rows, :], part.at[g, t, rows, :]
        return line_send.at[g, half, e], line.at[g, half, e]

    def rs(g, a, dirn, idx, kind):
        e = 2 if kind == 0 else (1 if dirn > 0 else 3)
        first = 0 if (kind != 1) == (dirn > 0) else QUARTER
        w = g * 20 + (a * 2 + (dirn + 1) // 2) * 5 + idx
        src = rs_source(g, a, idx, e)[0].at[pl.ds(first, QUARTER), :]
        dst = far.at[w] if kind == 0 else near.at[w, pl.ds(first, QUARTER), :]
        return remote(
            src, dst, rs_send.at[w * 3 + kind], rs_recv.at[w * 3 + kind], {"seq": neighbour[a, dirn]}
        )

    def rs_any(ref, i, device):
        return remote(ref, ref, rs_send.at[i], rs_recv.at[i], device)

    def rs_first_sends(g, a, idx, e):
        if e == 2:
            rs(g, a, 1, idx, 0).start()
            rs(g, a, -1, idx, 0).start()
        elif e != 0:
            rs(g, a, 1 if e == 1 else -1, idx, 1).start()

    def partial_copy(g, t):
        i = g * UNITS + t
        return remote(part_sib.at[g, t], sib.at[g, t], p_send.at[i], p_recv.at[i], sibling)

    def add_sibling(g, t):
        partial_copy(g, t).wait_recv()
        total = part[g, t] + sib[g, t].astype(jnp.float32)
        part[g, t] = total
        send[g, t] = total.astype(jnp.bfloat16)

    def do_sum(g, t):
        dx, dz = ORDER[t]
        rs_first_sends(g, 1, 1 + dx, dz)
        rs_first_sends(g, 0, 1 + dz, dx)

    def do_dep(g, a, dirn, idx):
        rs(g, a, dirn, idx, 0).wait_recv()
        e, first = (1, 0) if dirn > 0 else (3, QUARTER)
        w = g * 20 + (a * 2 + (dirn + 1) // 2) * 5 + idx
        to_send, exact = rs_source(g, a, idx, e)
        rows = pl.ds(first, QUARTER)
        to_send[rows, :] = (exact[rows, :] + far[w].astype(jnp.float32)).astype(jnp.bfloat16)
        rs(g, a, dirn, idx, 2).start()

    def do_fin(g, a, idx):
        for dirn in (1, -1):
            for kind in (1, 2):
                rs(g, a, dirn, idx, kind).wait_recv()
        up, down = g * 20 + a * 10 + 5 + idx, g * 20 + a * 10 + idx
        exact = rs_source(g, a, idx, 0)[1]
        half = rs_half(a, idx)
        total = exact[...] + near[up].astype(jnp.float32) + near[down].astype(jnp.float32)
        if idx == 0:
            att[half * HALF : (half + 1) * HALF, :] = total
        else:
            line[g, half, idx - 1] = total
            line_send[g, half, idx - 1] = total.astype(jnp.bfloat16)
            rs_first_sends(g, 1 - a, 0, idx - 1)

    steps = {}
    for step, _, g, kind, args in schedule():
        steps.setdefault(step, []).append((kind, (g,) + args))

    def run_step(step):
        for kind, args in steps.get(step, []):
            {"sum": do_sum, "dep": do_dep, "fin": do_fin}[kind](*args)

    def queries_copy(i, shard, batch, group):
        rows = pl.ds(pl.multiple_of(batch * 4 * ROWS, ROWS), 4 * ROWS)
        cols = pl.ds(pl.multiple_of(shard * 512 + group * 256, 256), 256)
        j = i * 2 + shard
        return remote(q_own.at[rows, cols], q_sib.at[rows, cols], q_sems.at[j], q_sems.at[16 + j], sibling)

    def project(i, batch, group):
        code_x, code_z = digits(CODES_X, batch), digits(CODES_Z, batch)
        for m in range(4):
            dx, dz = lax.rem(lax.div(code_x, 4**m), 4), lax.rem(lax.div(code_z, 4**m), 4)
            slot = lax.rem(x + dx, 4) * 4 + lax.rem(z + dz, 4)
            stage[m * ROWS : (m + 1) * ROWS, :] = normed[slot]
        rows = pl.ds(pl.multiple_of(batch * 4 * ROWS, ROWS), 4 * ROWS)
        got = [
            jnp.dot(
                stage[...], w_in[2 + shard, :, pl.ds(pl.multiple_of(group * 256, 256), 256)],
                preferred_element_type=jnp.float32,
            )
            for shard in range(2)
        ]
        for shard in range(2):
            cols = pl.ds(pl.multiple_of(shard * 512 + group * 256, 256), 256)
            q_own[rows, cols] = silu_of(got[shard], 0.5).astype(jnp.bfloat16)
            queries_copy(i, shard, batch, group).start()

    half_scale = 0.5 / math.sqrt(HEAD)

    def unit(t, group, code_x, code_z):
        blocks = []
        for n in range(2):
            dx, dz = lax.rem(lax.div(code_x, 4**n), 4), lax.rem(lax.div(code_z, 4**n), 4)
            chip = lax.rem(x + dx, 4) * 4 + lax.rem(z + dz, 4)
            rows = pl.ds(pl.multiple_of((t + n) * ROWS, ROWS), ROWS)
            blocks.append((0, t + n, rows, owner_ref[2 * chip + core]))
            blocks.append((1, t + n, rows, owner_ref[2 * chip + 1 - core]))
        starts = [shard * 512 + group * 256 + h * HEAD for shard in range(2) for h in range(2)]
        heads = [slice(start, start + HEAD) for start in starts]
        items = [(block, i) for block in blocks for i in range(len(heads))]

        def scores_of(i):
            (sibs, _, rows, owner), cols = items[i][0], heads[items[i][1]]
            return lax.dot_general(
                keys[owner, :, cols], (q_own, q_sib)[sibs][rows, cols],
                (((1,), (1,)), ((), ())), preferred_element_type=jnp.float32,
            )

        pending = [scores_of(0), scores_of(1)]
        for i, ((sibs, at, rows, owner), n) in enumerate(items):
            cols = heads[n]
            if i + 2 < len(items):
                pending.append(scores_of(i + 2))
            weights = silu_of(pending.pop(0), half_scale).astype(jnp.bfloat16)
            got = lax.dot_general(
                weights, values[owner, :, cols],
                (((0,), (0,)), ((), ())), preferred_element_type=jnp.float32,
            )
            if sibs == 0:
                part[0, at, :, cols] = got
            else:
                part_sib[0, at, :, cols] = got.astype(jnp.bfloat16)

    def early_2():
        early([4, 5])
        ag_3()

    def early_3():
        early([6, 7])

    extras = {
        0: [early_2, ag_4], 1: [early_3, ag_5], 2: [late_1], 3: [ag_6], 5: [ag_7],
        12: [late_2], 14: [late_3],
    }

    def step_body(s, carry):
        to_project, to_attend, to_add = carry

        @pl.when(s == 4)
        def _():
            early_rest([4, 5, 6, 7])

        @pl.when((lax.rem(s, 2) == 0) & (s < STEPS))
        def _():
            project(lax.div(s, 2), lax.rem(to_project, 4), lax.rem(lax.div(to_project, 4), 2))

        @pl.when((s >= 1) & (s <= STEPS))
        def _():
            it = s - 1
            batch, group = lax.rem(to_attend, 4), lax.rem(lax.div(to_attend, 4), 2)
            second = lax.rem(it, 2)
            t = batch * 4 + second * 2

            @pl.when(second == 0)
            def _():
                for shard in range(2):
                    queries_copy(lax.div(it, 2), shard, batch, group).wait_recv()

            code_x = shifted(digits(CODES_X, batch), 16, second)
            code_z = shifted(digits(CODES_Z, batch), 16, second)
            for g in range(2):

                @pl.when(group == g)
                def _(g=g):
                    unit(t, g, code_x, code_z)

            @pl.when(group == 1)
            def _():
                partial_copy(0, t).start()
                partial_copy(0, t + 1).start()

        @pl.when((s >= 2) & (lax.rem(lax.div(to_add, 4), 2) == 1))
        def _():
            t = lax.rem(to_add, 4) * 4 + lax.rem(s, 2) * 2
            add_sibling(0, t)
            add_sibling(0, t + 1)

        for k in range(STEPS + 2):
            todo = extras.get(k, [])
            if todo or k in steps:

                @pl.when(s == k)
                def _(k=k, todo=todo):
                    for action in todo:
                        action()
                    run_step(k)

        odd, late_enough, later = lax.rem(s, 2), lax.div(s + 15, 16), lax.div(s + 13, 16)
        return (
            shifted(to_project, 8, odd),
            shifted(to_attend, 8, (1 - odd) * late_enough),
            shifted(to_add, 8, odd * later),
        )

    lax.fori_loop(0, STEPS + 2, step_body, (CODE, CODE, CODE))
    late = [step for step in sorted(steps) if step > STEPS + 1]
    run_step(late[0])
    late_4()
    make_gate()
    for step in late[1:]:
        run_step(step)

    def norm_att(rows):
        gated = normalize(att[rows, :]) * gate[rows, :].astype(jnp.float32)
        gate[rows, :] = gated.astype(jnp.bfloat16)

    by_rows(ROWS, norm_att)

    branch = jnp.dot(
        gate[...], w_out[...].reshape(WIDTH, WIDTH), preferred_element_type=jnp.float32
    )
    out_ref[...] = (cand_ref[...].astype(jnp.float32) + branch).astype(jnp.bfloat16)

    def sent(count, copy_of):
        def one(i, carry):
            copy_of(i).wait_send()
            return carry

        lax.fori_loop(0, count, one, 0)

    east = {"seq": neighbour[0, 1]}
    for rows, first in ((HALF, 0), (QUARTER, 1)):
        block = normed.at[0, pl.ds(0, rows), :]
        sent(20, lambda i, block=block, first=first: ag_any(block, 2 * i + first, east))
    sent(60, lambda i: rs_any(far.at[0], i, east))
    for which in range(6):
        sent(CHUNKS, lambda chunk, which=which: weight(which, chunk))
        weight(which, CHUNKS).wait_send()
    for shard in range(2):
        sent(8, lambda i, shard=shard: queries_copy(i, shard, 0, 0))
    sent(UNITS, lambda t: partial_copy(0, t))


def per_device(candidates, block_user, hist_len, key_cache, value_cache, w_in, w_out):
    users, span, width = key_cache.shape[1:]
    vmem = pl.BlockSpec(memory_space=pltpu.VMEM)
    smem = pl.BlockSpec(memory_space=pltpu.SMEM)
    anywhere = pl.BlockSpec(memory_space=pl.ANY)
    bf16, f32 = jnp.bfloat16, jnp.float32
    dma = pltpu.SemaphoreType.DMA
    updated = pl.pallas_call(
        layer_kernel,
        out_shape=jax.ShapeDtypeStruct((ROWS, width), bf16),
        in_specs=[smem, smem, vmem, anywhere, anywhere, anywhere, anywhere],
        out_specs=vmem,
        scratch_shapes=[
            pltpu.VMEM((users, span, width), bf16),
            pltpu.VMEM((users, span, width), bf16),
            pltpu.VMEM((4,) + w_in.shape, bf16),
            pltpu.VMEM((4,) + w_out.shape, bf16),
            pltpu.VMEM((UNITS, ROWS, width), bf16),
            pltpu.VMEM((4 * ROWS, width), bf16),
            pltpu.VMEM((UNITS * ROWS, width), bf16),
            pltpu.VMEM((UNITS * ROWS, width), bf16),
            pltpu.VMEM((1, UNITS, ROWS, width), f32),
            pltpu.VMEM((1, UNITS, ROWS, width), bf16),
            pltpu.VMEM((1, UNITS, ROWS, width), bf16),
            pltpu.VMEM((1, UNITS, ROWS, width), bf16),
            pltpu.VMEM((20, QUARTER, width), bf16),
            pltpu.VMEM((20, HALF, width), bf16),
            pltpu.VMEM((1, 2, 4, HALF, width), f32),
            pltpu.VMEM((1, 2, 4, HALF, width), bf16),
            pltpu.VMEM((ROWS, width), f32),
            pltpu.VMEM((ROWS, width), bf16),
            dma((4,)),
            dma((40,)),
            dma((40,)),
            dma((6 * (CHUNKS + 1),)),
            dma((6 * (CHUNKS + 1),)),
            dma((32,)),
            dma((UNITS,)),
            dma((UNITS,)),
            dma((60,)),
            dma((60,)),
        ],
        compiler_params=pltpu.CompilerParams(
            collective_id=0, has_side_effects=True, vmem_limit_bytes=60 << 20
        ),
        name="layer",
    )(
        block_user[0], hist_len[0], candidates[0, 0], key_cache[0], value_cache[0], w_in, w_out
    )
    return updated.reshape(candidates.shape)


def solution(mesh):
    in_specs = (
        P("grp", "seq", None, None),
        P("grp", None),
        P("grp", None),
        P("grp", None, "seq", None),
        P("grp", None, "seq", None),
        P(None, "grp"),
        P("grp", None),
    )
    out_specs = P("grp", "seq", None, None)
    return jax.shard_map(
        per_device, mesh=mesh, in_specs=in_specs, out_specs=out_specs, check_vma=False
    )
```

```python
import math

import jax
import jax.numpy as jnp
from jax import lax
from jax.experimental import pallas as pl
from jax.experimental.pallas import tpu as pltpu
from jax.sharding import PartitionSpec as P

HEADS = 8
EPSILON = 1e-05
SIDE = 4
ROWS = 128
HALF = 64
QUARTER = 32
WIDTH = 1024
HEAD = WIDTH // HEADS
UNITS = SIDE * SIDE
ROW_CHUNKS = 4
CHUNKS = 2 * ROW_CHUNKS
STEPS = 16
LAG = 2

ORDER = [
    (0, 0), (1, 0), (3, 0), (0, 3),
    (1, 1), (3, 3), (1, 3), (0, 1),
    (2, 2), (2, 1), (1, 2), (2, 3),
    (3, 2), (2, 0), (0, 2), (3, 1),
]
PLACE = {offset: t for t, offset in enumerate(ORDER)}
CODES_X = [sum(dx * 4**t for t, (dx, _) in enumerate(ORDER[i : i + 8])) for i in (0, 8)]
CODES_Z = [sum(dz * 4**t for t, (_, dz) in enumerate(ORDER[i : i + 8])) for i in (0, 8)]
PARTS = [(0, 0), (1, 0), (1, 1), (2, 0), (2, 1), (3, 0), (3, 1), (0, 1)]
CODE = sum((batch + 4 * group) * 8**i for i, (batch, group) in enumerate(PARTS))


def shifted(code, base, when):
    return code + when * (lax.div(code, base) - code)


def digits(codes, batch):
    high = lax.div(batch, 2)
    return shifted(codes[0] + high * (codes[1] - codes[0]), 256, lax.rem(batch, 2))


def normalize(values):
    mean = jnp.mean(values, axis=-1, keepdims=True)
    centered = values - mean
    variance = jnp.mean(centered * centered, axis=-1, keepdims=True)
    return centered * lax.rsqrt(variance + EPSILON)


def silu_of(values, half_scale):
    half = values * half_scale
    return half + half * jnp.tanh(half)


def place_of(a, along, across):
    return PLACE[(along % 4, across) if a == 0 else (across, along % 4)]


def schedule():
    ready = {}
    for it in range(STEPS):
        batch, group = PARTS[it // 2]
        for n in range(2 * group):
            ready[0, 4 * batch + it % 2 * 2 + n] = it + 2
    events = [(step, 0, g, "sum", (t,)) for (g, t), step in ready.items()]
    for g in range(1):
        done = {}
        for a in (0, 1):
            for d in range(4):
                steps = []
                for dirn, e in ((1, 1), (-1, 3)):
                    step = max(ready[g, place_of(a, e, d)], ready[g, place_of(a, 2, d)] + LAG)
                    events.append((step, 1, g, "dep", (a, dirn, 1 + d)))
                    steps.append(step + LAG)
                done[a, d] = max([ready[g, place_of(a, 0, d)]] + steps)
                events.append((done[a, d], 2, g, "fin", (a, 1 + d)))
        for a in (0, 1):
            b = 1 - a
            steps = []
            for dirn, e in ((1, 1), (-1, 3)):
                step = max(done[b, e], done[b, 2] + LAG)
                events.append((step, 3, g, "dep", (a, dirn, 0)))
                steps.append(step + LAG)
            events.append((max([done[b, 0]] + steps), 4, g, "fin", (a, 0)))
    return sorted(events)


def layer_kernel(
    owner_ref, length_ref, cand_ref, k_hbm, v_hbm, win_hbm, wout_hbm, out_ref,
    keys, values, w_in, w_out, normed, stage, q_own, q_sib, part, part_sib, sib, send, far, near,
    line, line_send, att, gate,
    local_sem, ag_send, ag_recv, w_send, w_recv, q_sems, p_send, p_recv, rs_send, rs_recv,
):
    seq = lax.axis_index("seq")
    y = lax.axis_index("grp")
    core = lax.rem(seq, 2)
    z = lax.rem(lax.div(seq, 2), 4)
    x = lax.div(seq, 8)
    span = keys.shape[1]
    users = keys.shape[0]

    def at_chip(dx, dz):
        return (lax.rem(x + dx, 4) * 4 + lax.rem(z + dz, 4)) * 2 + core

    neighbour = {
        (0, 1): at_chip(1, 0), (0, -1): at_chip(3, 0), (1, 1): at_chip(0, 1), (1, -1): at_chip(0, 3),
    }
    sibling = {"seq": seq - core + (1 - core)}
    outer_y = 3 - y
    inner_y = y + 1 - 2 * lax.rem(y, 2)
    rest_y = 3 - inner_y

    def remote(src, dst, send_sem, recv_sem, device):
        return pltpu.make_async_remote_copy(
            src_ref=src, dst_ref=dst, send_sem=send_sem, recv_sem=recv_sem,
            device_id=device, device_id_type=pl.DeviceIdType.MESH,
        )

    barrier = pltpu.get_barrier_semaphore()
    peers = [{"seq": n} for n in neighbour.values()] + [sibling, {"grp": outer_y}, {"grp": inner_y}]
    for peer in peers:
        pl.semaphore_signal(barrier, inc=1, device_id=peer, device_id_type=pl.DeviceIdType.MESH)
    copies = [
        pltpu.make_async_copy(v_hbm, values, local_sem.at[0]),
        pltpu.make_async_copy(k_hbm, keys, local_sem.at[1]),
        pltpu.make_async_copy(win_hbm, w_in.at[y], local_sem.at[2]),
        pltpu.make_async_copy(wout_hbm, w_out.at[y], local_sem.at[3]),
    ]
    own_slot = x * 4 + z

    def by_rows(count, action):
        action(pl.ds(0, count))

    def norm_rows(rows):
        normed[own_slot, rows, :] = normalize(cand_ref[rows, :].astype(jnp.float32)).astype(jnp.bfloat16)

    by_rows(ROWS, norm_rows)
    pl.semaphore_wait(barrier, len(peers))

    in_half = w_in.shape[1] // 2
    in_rows = in_half // ROW_CHUNKS
    out_half = w_out.shape[1] // 2

    def weight(which, chunk, receiving=False):
        is_in = not (isinstance(chunk, int) and chunk == CHUNKS)
        array, hbm = (w_in, win_hbm) if is_in else (w_out, wout_hbm)
        half, rows = (in_half, in_rows) if is_in else (out_half, out_half)
        first = chunk % ROW_CHUNKS * rows if is_in else 0
        cols = pl.ds(chunk // ROW_CHUNKS * 256, 256) if is_in else pl.ds(0, WIDTH)
        side = core
        if which < 3:
            to = (outer_y, inner_y, inner_y if is_in else outer_y)[which]
            shard = (y, y, outer_y if is_in else inner_y)[which]
            if receiving:
                shard = (outer_y, inner_y, rest_y)[which]
            device = {"grp": to}
        else:
            shard = (outer_y, inner_y, rest_y)[which - 3]
            device = sibling
            if receiving:
                side = 1 - core
        rows_at = pl.ds(pl.multiple_of(side * half + first, 16), rows)
        dst = array.at[shard, rows_at, cols]
        src = hbm.at[rows_at, cols] if which < 2 and not receiving else dst
        i = which * (CHUNKS + 1) + chunk
        return remote(src, dst, w_send.at[i], w_recv.at[i], device)

    def each(chunks, action):
        for chunk in chunks:
            action(chunk)

    def start_own(which, chunks):
        each(chunks, lambda chunk: weight(which, chunk).start())

    def take(which, chunks):
        def one(chunk):
            weight(which, chunk, True).wait_recv()
            if which == (1 if chunks is out_chunks else 0):
                weight(2, chunk).start()
            weight(which + 3, chunk).start()

        each(chunks, one)

    def take_sibling(which, chunks):
        each(chunks, lambda chunk: weight(which, chunk, True).wait_recv())

    in_chunks = range(CHUNKS)
    out_chunks = [CHUNKS]

    def ag(a, dirn, idx, is_far, receiving=False):
        half = 0 if (a == 0) == (idx == 0) else 1
        d = max(idx - 1, 0)
        along = (-dirn if is_far else 0) - (dirn if receiving else 0)
        dx, dz = (along, d) if a == 0 else (d, along)
        slot = lax.rem(x + dx % 4, 4) * 4 + lax.rem(z + dz % 4, 4)
        first, count = half * HALF, HALF
        if is_far:
            first, count = first + (0 if dirn > 0 else QUARTER), QUARTER
        ref = normed.at[slot, pl.ds(first, count), :]
        i = ((a * 2 + (dirn + 1) // 2) * 5 + idx) * 2 + int(is_far)
        return remote(ref, ref, ag_send.at[i], ag_recv.at[i], {"seq": neighbour[a, dirn]})

    def ag_any(ref, i, device):
        return remote(ref, ref, ag_send.at[i], ag_recv.at[i], device)

    ways = [(a, dirn) for a in (0, 1) for dirn in (1, -1)]

    def ag_start(idxs, is_far):
        for idx in idxs:
            for a, dirn in ways:
                ag(a, dirn, idx, is_far).start()

    def ag_take(idxs, is_far):
        for idx in idxs:
            for a, dirn in ways:
                ag(a, dirn, idx, is_far, True).wait_recv()

    def ag_1():
        ag_take([0], False)
        ag_start([0], True)
        ag_start([2, 4], False)

    def ag_2():
        ag_take([1], False)
        ag_start([1], True)

    def ag_3():
        ag_take([0], True)
        ag_start([3], False)

    def ag_4():
        ag_take([2, 4], False)
        ag_start([2, 4], True)

    def ag_5():
        ag_take([1], True)

    def ag_6():
        ag_take([3], False)
        ag_start([3], True)

    def ag_7():
        ag_take([2, 4], True)
        ag_take([3], True)

    @pl.when(y >= 2)
    def _():
        def both(chunk):
            weight(0, chunk).start()
            weight(1, chunk).start()

        each(in_chunks, both)

    ag_start([0, 1], False)

    @pl.when(y < 2)
    def _():
        start_own(0, in_chunks)

    for copy in copies:
        copy.start()
    for copy in copies:
        copy.wait()
    offset = seq * span

    def mask_user(u, carry):
        rows = lax.broadcasted_iota(jnp.int32, (span, HEAD), 0)
        keep = jnp.where(rows < length_ref[u] - offset, 1.0, 0.0).astype(jnp.bfloat16)
        for h in range(HEADS):
            cols = slice(h * HEAD, (h + 1) * HEAD)
            values[u, :, cols] = values[u, :, cols] * keep
        return carry

    lax.fori_loop(0, users, mask_user, 0)

    def early(chunks):
        @pl.when(y < 2)
        def _():
            take(0, chunks)

        @pl.when(y >= 2)
        def _():
            take(1, chunks)

    def early_rest(chunks):
        @pl.when(y < 2)
        def _():
            take(2, chunks)
            take_sibling(3, chunks)
            take_sibling(5, chunks)

        @pl.when(y >= 2)
        def _():
            take_sibling(4, chunks)

    early([0, 1])
    ag_1()
    early([2, 3])
    ag_2()
    ag_3()
    early([4, 5])
    early_rest([0, 1, 2, 3])

    def late_1():
        @pl.when(y < 2)
        def _():
            start_own(1, in_chunks)

        @pl.when(y >= 2)
        def _():
            take(0, in_chunks)

        start_own(0, out_chunks)
        start_own(1, out_chunks)

    def late_2():
        @pl.when(y < 2)
        def _():
            take(1, in_chunks)

        @pl.when(y >= 2)
        def _():
            take(2, in_chunks)

    def late_3():
        take(1, out_chunks)
        take(0, out_chunks)

    def late_4():
        take(2, out_chunks)
        for which in (3, 4, 5):
            take_sibling(which, out_chunks)

        @pl.when(y < 2)
        def _():
            take_sibling(4, in_chunks)

        @pl.when(y >= 2)
        def _():
            take_sibling(3, in_chunks)
            take_sibling(5, in_chunks)

    def make_gate():
        own = normed[own_slot]
        for shard in (0, 1):
            got = jnp.dot(own, w_in[shard], preferred_element_type=jnp.float32)
            gate[:, shard * 512 : (shard + 1) * 512] = silu_of(got, 0.5).astype(jnp.bfloat16)

    def rs_half(a, idx):
        return 1 - a if idx > 0 else a

    def rs_source(g, a, idx, e):
        half = rs_half(a, idx)
        if idx > 0:
            t = place_of(a, e, idx - 1)
            rows = pl.ds(half * HALF, HALF)
            return send.at[g, t, rows, :], part.at[g, t, rows, :]
        return line_send.at[g, half, e], line.at[g, half, e]

    def rs(g, a, dirn, idx, kind):
        e = 2 if kind == 0 else (1 if dirn > 0 else 3)
        first = 0 if (kind != 1) == (dirn > 0) else QUARTER
        w = g * 20 + (a * 2 + (dirn + 1) // 2) * 5 + idx
        src = rs_source(g, a, idx, e)[0].at[pl.ds(first, QUARTER), :]
        dst = far.at[w] if kind == 0 else near.at[w, pl.ds(first, QUARTER), :]
        return remote(
            src, dst, rs_send.at[w * 3 + kind], rs_recv.at[w * 3 + kind], {"seq": neighbour[a, dirn]}
        )

    def rs_any(ref, i, device):
        return remote(ref, ref, rs_send.at[i], rs_recv.at[i], device)

    def rs_first_sends(g, a, idx, e):
        if e == 2:
            rs(g, a, 1, idx, 0).start()
            rs(g, a, -1, idx, 0).start()
        elif e != 0:
            rs(g, a, 1 if e == 1 else -1, idx, 1).start()

    def partial_copy(g, t):
        i = g * UNITS + t
        return remote(part_sib.at[g, t], sib.at[g, t], p_send.at[i], p_recv.at[i], sibling)

    def add_sibling(g, t):
        partial_copy(g, t).wait_recv()
        total = part[g, t] + sib[g, t].astype(jnp.float32)
        part[g, t] = total
        send[g, t] = total.astype(jnp.bfloat16)

    def do_sum(g, t):
        dx, dz = ORDER[t]
        rs_first_sends(g, 1, 1 + dx, dz)
        rs_first_sends(g, 0, 1 + dz, dx)

    def do_dep(g, a, dirn, idx):
        rs(g, a, dirn, idx, 0).wait_recv()
        e, first = (1, 0) if dirn > 0 else (3, QUARTER)
        w = g * 20 + (a * 2 + (dirn + 1) // 2) * 5 + idx
        to_send, exact = rs_source(g, a, idx, e)
        rows = pl.ds(first, QUARTER)
        to_send[rows, :] = (exact[rows, :] + far[w].astype(jnp.float32)).astype(jnp.bfloat16)
        rs(g, a, dirn, idx, 2).start()

    def do_fin(g, a, idx):
        for dirn in (1, -1):
            for kind in (1, 2):
                rs(g, a, dirn, idx, kind).wait_recv()
        up, down = g * 20 + a * 10 + 5 + idx, g * 20 + a * 10 + idx
        exact = rs_source(g, a, idx, 0)[1]
        half = rs_half(a, idx)
        total = exact[...] + near[up].astype(jnp.float32) + near[down].astype(jnp.float32)
        if idx == 0:
            att[half * HALF : (half + 1) * HALF, :] = total
        else:
            line[g, half, idx - 1] = total
            line_send[g, half, idx - 1] = total.astype(jnp.bfloat16)
            rs_first_sends(g, 1 - a, 0, idx - 1)

    steps = {}
    for step, _, g, kind, args in schedule():
        steps.setdefault(step, []).append((kind, (g,) + args))

    def run_step(step):
        for kind, args in steps.get(step, []):
            {"sum": do_sum, "dep": do_dep, "fin": do_fin}[kind](*args)

    def queries_copy(i, shard, batch, group):
        rows = pl.ds(pl.multiple_of(batch * 4 * ROWS, ROWS), 4 * ROWS)
        cols = pl.ds(pl.multiple_of(shard * 512 + group * 256, 256), 256)
        j = i * 2 + shard
        return remote(q_own.at[rows, cols], q_sib.at[rows, cols], q_sems.at[j], q_sems.at[16 + j], sibling)

    def project(i, batch, group):
        code_x, code_z = digits(CODES_X, batch), digits(CODES_Z, batch)
        for m in range(4):
            dx, dz = lax.rem(lax.div(code_x, 4**m), 4), lax.rem(lax.div(code_z, 4**m), 4)
            slot = lax.rem(x + dx, 4) * 4 + lax.rem(z + dz, 4)
            stage[m * ROWS : (m + 1) * ROWS, :] = normed[slot]
        rows = pl.ds(pl.multiple_of(batch * 4 * ROWS, ROWS), 4 * ROWS)
        got = [
            jnp.dot(
                stage[...], w_in[2 + shard, :, pl.ds(pl.multiple_of(group * 256, 256), 256)],
                preferred_element_type=jnp.float32,
            )
            for shard in range(2)
        ]
        for shard in range(2):
            cols = pl.ds(pl.multiple_of(shard * 512 + group * 256, 256), 256)
            q_own[rows, cols] = silu_of(got[shard], 0.5).astype(jnp.bfloat16)
            queries_copy(i, shard, batch, group).start()

    half_scale = 0.5 / math.sqrt(HEAD)

    def unit(t, group, code_x, code_z):
        blocks = []
        for n in range(2):
            dx, dz = lax.rem(lax.div(code_x, 4**n), 4), lax.rem(lax.div(code_z, 4**n), 4)
            chip = lax.rem(x + dx, 4) * 4 + lax.rem(z + dz, 4)
            rows = pl.ds(pl.multiple_of((t + n) * ROWS, ROWS), ROWS)
            blocks.append((0, t + n, rows, owner_ref[2 * chip + core]))
            blocks.append((1, t + n, rows, owner_ref[2 * chip + 1 - core]))
        starts = [shard * 512 + group * 256 + h * HEAD for shard in range(2) for h in range(2)]
        heads = [slice(start, start + HEAD) for start in starts]
        items = [(block, i) for block in blocks for i in range(len(heads))]

        def scores_of(i):
            (sibs, _, rows, owner), cols = items[i][0], heads[items[i][1]]
            return lax.dot_general(
                keys[owner, :, cols], (q_own, q_sib)[sibs][rows, cols],
                (((1,), (1,)), ((), ())), preferred_element_type=jnp.float32,
            )

        pending = [scores_of(0), scores_of(1)]
        for i, ((sibs, at, rows, owner), n) in enumerate(items):
            cols = heads[n]
            if i + 2 < len(items):
                pending.append(scores_of(i + 2))
            weights = silu_of(pending.pop(0), half_scale).astype(jnp.bfloat16)
            got = lax.dot_general(
                weights, values[owner, :, cols],
                (((0,), (0,)), ((), ())), preferred_element_type=jnp.float32,
            )
            if sibs == 0:
                part[0, at, :, cols] = got
            else:
                part_sib[0, at, :, cols] = got.astype(jnp.bfloat16)

    def early_3():
        early([6, 7])

    extras = {
        0: [early_3, ag_4], 1: [ag_5], 2: [ag_6, late_1], 4: [ag_7],
        12: [late_2], 14: [late_3],
    }

    def step_body(s, carry):
        to_project, to_attend, to_add = carry

        @pl.when(s == 4)
        def _():
            early_rest([4, 5, 6, 7])

        @pl.when((lax.rem(s, 2) == 0) & (s < STEPS))
        def _():
            project(lax.div(s, 2), lax.rem(to_project, 4), lax.rem(lax.div(to_project, 4), 2))

        @pl.when((s >= 1) & (s <= STEPS))
        def _():
            it = s - 1
            batch, group = lax.rem(to_attend, 4), lax.rem(lax.div(to_attend, 4), 2)
            second = lax.rem(it, 2)
            t = batch * 4 + second * 2

            @pl.when(second == 0)
            def _():
                for shard in range(2):
                    queries_copy(lax.div(it, 2), shard, batch, group).wait_recv()

            code_x = shifted(digits(CODES_X, batch), 16, second)
            code_z = shifted(digits(CODES_Z, batch), 16, second)
            for g in range(2):

                @pl.when(group == g)
                def _(g=g):
                    unit(t, g, code_x, code_z)

            @pl.when(group == 1)
            def _():
                partial_copy(0, t).start()
                partial_copy(0, t + 1).start()

        @pl.when((s >= 2) & (lax.rem(lax.div(to_add, 4), 2) == 1))
        def _():
            t = lax.rem(to_add, 4) * 4 + lax.rem(s, 2) * 2
            add_sibling(0, t)
            add_sibling(0, t + 1)

        for k in range(STEPS + 2):
            todo = extras.get(k, [])
            if todo or k in steps:

                @pl.when(s == k)
                def _(k=k, todo=todo):
                    for action in todo:
                        action()
                    run_step(k)

        odd, late_enough, later = lax.rem(s, 2), lax.div(s + 15, 16), lax.div(s + 13, 16)
        return (
            shifted(to_project, 8, odd),
            shifted(to_attend, 8, (1 - odd) * late_enough),
            shifted(to_add, 8, odd * later),
        )

    lax.fori_loop(0, STEPS + 2, step_body, (CODE, CODE, CODE))
    late = [step for step in sorted(steps) if step > STEPS + 1]
    run_step(late[0])
    late_4()
    make_gate()
    for step in late[1:]:
        run_step(step)

    def norm_att(rows):
        gated = normalize(att[rows, :]) * gate[rows, :].astype(jnp.float32)
        gate[rows, :] = gated.astype(jnp.bfloat16)

    by_rows(ROWS, norm_att)

    branch = jnp.dot(
        gate[...], w_out[...].reshape(WIDTH, WIDTH), preferred_element_type=jnp.float32
    )
    out_ref[...] = (cand_ref[...].astype(jnp.float32) + branch).astype(jnp.bfloat16)

    def sent(count, copy_of):
        for i in range(count):
            copy_of(i).wait_send()

    east = {"seq": neighbour[0, 1]}
    for rows, first in ((HALF, 0), (QUARTER, 1)):
        block = normed.at[0, pl.ds(0, rows), :]
        sent(20, lambda i, block=block, first=first: ag_any(block, 2 * i + first, east))
    sent(60, lambda i: rs_any(far.at[0], i, east))
    for which in range(6):
        sent(CHUNKS, lambda chunk, which=which: weight(which, chunk))
        weight(which, CHUNKS).wait_send()
    for shard in range(2):
        sent(8, lambda i, shard=shard: queries_copy(i, shard, 0, 0))
    sent(UNITS, lambda t: partial_copy(0, t))


def per_device(candidates, block_user, hist_len, key_cache, value_cache, w_in, w_out):
    users, span, width = key_cache.shape[1:]
    vmem = pl.BlockSpec(memory_space=pltpu.VMEM)
    smem = pl.BlockSpec(memory_space=pltpu.SMEM)
    anywhere = pl.BlockSpec(memory_space=pl.ANY)
    bf16, f32 = jnp.bfloat16, jnp.float32
    dma = pltpu.SemaphoreType.DMA
    updated = pl.pallas_call(
        layer_kernel,
        out_shape=jax.ShapeDtypeStruct((ROWS, width), bf16),
        in_specs=[smem, smem, vmem, anywhere, anywhere, anywhere, anywhere],
        out_specs=vmem,
        scratch_shapes=[
            pltpu.VMEM((users, span, width), bf16),
            pltpu.VMEM((users, span, width), bf16),
            pltpu.VMEM((4,) + w_in.shape, bf16),
            pltpu.VMEM((4,) + w_out.shape, bf16),
            pltpu.VMEM((UNITS, ROWS, width), bf16),
            pltpu.VMEM((4 * ROWS, width), bf16),
            pltpu.VMEM((UNITS * ROWS, width), bf16),
            pltpu.VMEM((UNITS * ROWS, width), bf16),
            pltpu.VMEM((1, UNITS, ROWS, width), f32),
            pltpu.VMEM((1, UNITS, ROWS, width), bf16),
            pltpu.VMEM((1, UNITS, ROWS, width), bf16),
            pltpu.VMEM((1, UNITS, ROWS, width), bf16),
            pltpu.VMEM((20, QUARTER, width), bf16),
            pltpu.VMEM((20, HALF, width), bf16),
            pltpu.VMEM((1, 2, 4, HALF, width), f32),
            pltpu.VMEM((1, 2, 4, HALF, width), bf16),
            pltpu.VMEM((ROWS, width), f32),
            pltpu.VMEM((ROWS, width), bf16),
            dma((4,)),
            dma((40,)),
            dma((40,)),
            dma((6 * (CHUNKS + 1),)),
            dma((6 * (CHUNKS + 1),)),
            dma((32,)),
            dma((UNITS,)),
            dma((UNITS,)),
            dma((60,)),
            dma((60,)),
        ],
        compiler_params=pltpu.CompilerParams(
            collective_id=0, has_side_effects=True, vmem_limit_bytes=60 << 20
        ),
        name="layer",
    )(
        block_user[0], hist_len[0], candidates[0, 0], key_cache[0], value_cache[0], w_in, w_out
    )
    return updated.reshape(candidates.shape)


def solution(mesh):
    in_specs = (
        P("grp", "seq", None, None),
        P("grp", None),
        P("grp", None),
        P("grp", None, "seq", None),
        P("grp", None, "seq", None),
        P(None, "grp"),
        P("grp", None),
    )
    out_specs = P("grp", "seq", None, None)
    return jax.shard_map(
        per_device, mesh=mesh, in_specs=in_specs, out_specs=out_specs, check_vma=False
    )
```

```python
import math

import jax
import jax.numpy as jnp
from jax import lax
from jax.experimental import pallas as pl
from jax.experimental.pallas import tpu as pltpu
from jax.sharding import PartitionSpec as P

HEADS = 8
EPSILON = 1e-05
SIDE = 4
ROWS = 128
HALF = 64
QUARTER = 32
WIDTH = 1024
HEAD = WIDTH // HEADS
UNITS = SIDE * SIDE
ROW_CHUNKS = 4
CHUNKS = 2 * ROW_CHUNKS
STEPS = 16
LAG = 2

ORDER = [
    (0, 0), (1, 0), (3, 0), (0, 3),
    (1, 1), (3, 3), (1, 3), (0, 1),
    (2, 2), (2, 1), (1, 2), (2, 3),
    (3, 2), (2, 0), (0, 2), (3, 1),
]
PLACE = {offset: t for t, offset in enumerate(ORDER)}
CODES_X = [sum(dx * 4**t for t, (dx, _) in enumerate(ORDER[i : i + 8])) for i in (0, 8)]
CODES_Z = [sum(dz * 4**t for t, (_, dz) in enumerate(ORDER[i : i + 8])) for i in (0, 8)]
PARTS = [(0, 0), (1, 0), (1, 1), (2, 0), (2, 1), (3, 0), (3, 1), (0, 1)]
CODE = sum((batch + 4 * group) * 8**i for i, (batch, group) in enumerate(PARTS))


def shifted(code, base, when):
    return code + when * (lax.div(code, base) - code)


def digits(codes, batch):
    high = lax.div(batch, 2)
    return shifted(codes[0] + high * (codes[1] - codes[0]), 256, lax.rem(batch, 2))


def normalize(values):
    mean = jnp.mean(values, axis=-1, keepdims=True)
    centered = values - mean
    variance = jnp.mean(centered * centered, axis=-1, keepdims=True)
    return centered * lax.rsqrt(variance + EPSILON)


def silu_of(values, half_scale):
    half = values * half_scale
    return half + half * jnp.tanh(half)


def place_of(a, along, across):
    return PLACE[(along % 4, across) if a == 0 else (across, along % 4)]


def schedule():
    ready = {}
    for it in range(STEPS):
        batch, group = PARTS[it // 2]
        for n in range(2 * group):
            ready[0, 4 * batch + it % 2 * 2 + n] = it + 2
    events = [(step, 0, g, "sum", (t,)) for (g, t), step in ready.items()]
    for g in range(1):
        done = {}
        for a in (0, 1):
            for d in range(4):
                steps = []
                for dirn, e in ((1, 1), (-1, 3)):
                    step = max(ready[g, place_of(a, e, d)], ready[g, place_of(a, 2, d)] + LAG)
                    events.append((step, 1, g, "dep", (a, dirn, 1 + d)))
                    steps.append(step + LAG)
                done[a, d] = max([ready[g, place_of(a, 0, d)]] + steps)
                events.append((done[a, d], 2, g, "fin", (a, 1 + d)))
        for a in (0, 1):
            b = 1 - a
            steps = []
            for dirn, e in ((1, 1), (-1, 3)):
                step = max(done[b, e], done[b, 2] + LAG)
                events.append((step, 3, g, "dep", (a, dirn, 0)))
                steps.append(step + LAG)
            events.append((max([done[b, 0]] + steps), 4, g, "fin", (a, 0)))
    return sorted(events)


def layer_kernel(
    owner_ref, length_ref, cand_ref, k_hbm, v_hbm, win_hbm, wout_hbm, out_ref,
    keys, values, w_in, w_out, normed, stage, q_own, q_sib, part, part_sib, sib, send, far, near,
    line, line_send, att, gate,
    local_sem, ag_send, ag_recv, w_send, w_recv, q_sems, p_send, p_recv, rs_send, rs_recv,
):
    seq = lax.axis_index("seq")
    y = lax.axis_index("grp")
    core = lax.rem(seq, 2)
    z = lax.rem(lax.div(seq, 2), 4)
    x = lax.div(seq, 8)
    span = keys.shape[1]
    users = keys.shape[0]

    def at_chip(dx, dz):
        return (lax.rem(x + dx, 4) * 4 + lax.rem(z + dz, 4)) * 2 + core

    neighbour = {
        (0, 1): at_chip(1, 0), (0, -1): at_chip(3, 0), (1, 1): at_chip(0, 1), (1, -1): at_chip(0, 3),
    }
    sibling = {"seq": seq - core + (1 - core)}
    outer_y = 3 - y
    inner_y = y + 1 - 2 * lax.rem(y, 2)
    rest_y = 3 - inner_y

    def remote(src, dst, send_sem, recv_sem, device):
        return pltpu.make_async_remote_copy(
            src_ref=src, dst_ref=dst, send_sem=send_sem, recv_sem=recv_sem,
            device_id=device, device_id_type=pl.DeviceIdType.MESH,
        )

    barrier = pltpu.get_barrier_semaphore()
    peers = [{"seq": n} for n in neighbour.values()] + [sibling, {"grp": outer_y}, {"grp": inner_y}]
    for peer in peers:
        pl.semaphore_signal(barrier, inc=1, device_id=peer, device_id_type=pl.DeviceIdType.MESH)
    copies = [
        pltpu.make_async_copy(v_hbm, values, local_sem.at[0]),
        pltpu.make_async_copy(k_hbm, keys, local_sem.at[1]),
        pltpu.make_async_copy(win_hbm, w_in.at[y], local_sem.at[2]),
        pltpu.make_async_copy(wout_hbm, w_out.at[y], local_sem.at[3]),
    ]
    own_slot = x * 4 + z

    def by_rows(count, action):
        action(pl.ds(0, count))

    def norm_rows(rows):
        normed[own_slot, rows, :] = normalize(cand_ref[rows, :].astype(jnp.float32)).astype(jnp.bfloat16)

    by_rows(ROWS, norm_rows)
    pl.semaphore_wait(barrier, len(peers))

    in_half = w_in.shape[1] // 2
    in_rows = in_half // ROW_CHUNKS
    out_half = w_out.shape[1] // 2

    def weight(which, chunk, receiving=False):
        is_in = not (isinstance(chunk, int) and chunk == CHUNKS)
        array, hbm = (w_in, win_hbm) if is_in else (w_out, wout_hbm)
        half, rows = (in_half, in_rows) if is_in else (out_half, out_half)
        first = chunk % ROW_CHUNKS * rows if is_in else 0
        cols = pl.ds(chunk // ROW_CHUNKS * 256, 256) if is_in else pl.ds(0, WIDTH)
        side = core
        if which < 3:
            to = (outer_y, inner_y, inner_y if is_in else outer_y)[which]
            shard = (y, y, outer_y if is_in else inner_y)[which]
            if receiving:
                shard = (outer_y, inner_y, rest_y)[which]
            device = {"grp": to}
        else:
            shard = (outer_y, inner_y, rest_y)[which - 3]
            device = sibling
            if receiving:
                side = 1 - core
        rows_at = pl.ds(pl.multiple_of(side * half + first, 16), rows)
        dst = array.at[shard, rows_at, cols]
        src = hbm.at[rows_at, cols] if which < 2 and not receiving else dst
        i = which * (CHUNKS + 1) + chunk
        return remote(src, dst, w_send.at[i], w_recv.at[i], device)

    def each(chunks, action):
        for chunk in chunks:
            action(chunk)

    def start_own(which, chunks):
        each(chunks, lambda chunk: weight(which, chunk).start())

    def take(which, chunks):
        def one(chunk):
            weight(which, chunk, True).wait_recv()
            if which == (1 if chunks is out_chunks else 0):
                weight(2, chunk).start()
            weight(which + 3, chunk).start()

        each(chunks, one)

    def take_sibling(which, chunks):
        each(chunks, lambda chunk: weight(which, chunk, True).wait_recv())

    in_chunks = range(CHUNKS)
    out_chunks = [CHUNKS]

    def ag(a, dirn, idx, is_far, receiving=False):
        half = 0 if (a == 0) == (idx == 0) else 1
        d = max(idx - 1, 0)
        along = (-dirn if is_far else 0) - (dirn if receiving else 0)
        dx, dz = (along, d) if a == 0 else (d, along)
        slot = lax.rem(x + dx % 4, 4) * 4 + lax.rem(z + dz % 4, 4)
        first, count = half * HALF, HALF
        if is_far:
            first, count = first + (0 if dirn > 0 else QUARTER), QUARTER
        ref = normed.at[slot, pl.ds(first, count), :]
        i = ((a * 2 + (dirn + 1) // 2) * 5 + idx) * 2 + int(is_far)
        return remote(ref, ref, ag_send.at[i], ag_recv.at[i], {"seq": neighbour[a, dirn]})

    def ag_any(ref, i, device):
        return remote(ref, ref, ag_send.at[i], ag_recv.at[i], device)

    ways = [(a, dirn) for a in (0, 1) for dirn in (1, -1)]

    def ag_start(idxs, is_far):
        for idx in idxs:
            for a, dirn in ways:
                ag(a, dirn, idx, is_far).start()

    def ag_take(idxs, is_far):
        for idx in idxs:
            for a, dirn in ways:
                ag(a, dirn, idx, is_far, True).wait_recv()

    def ag_1():
        ag_take([0], False)
        ag_start([0], True)
        ag_start([2, 4], False)

    def ag_2():
        ag_take([1], False)
        ag_start([1], True)

    def ag_3():
        ag_take([0], True)
        ag_start([3], False)

    def ag_4():
        ag_take([2, 4], False)
        ag_start([2, 4], True)

    def ag_5():
        ag_take([1], True)

    def ag_6():
        ag_take([3], False)
        ag_start([3], True)

    def ag_7():
        ag_take([2, 4], True)
        ag_take([3], True)

    @pl.when(y >= 2)
    def _():
        def both(chunk):
            weight(0, chunk).start()
            weight(1, chunk).start()

        each(in_chunks, both)

    ag_start([0, 1], False)

    @pl.when(y < 2)
    def _():
        start_own(0, in_chunks)

    for copy in copies:
        copy.start()
    for copy in copies:
        copy.wait()
    offset = seq * span

    def mask_user(u, carry):
        rows = lax.broadcasted_iota(jnp.int32, (span, HEAD), 0)
        keep = jnp.where(rows < length_ref[u] - offset, 1.0, 0.0).astype(jnp.bfloat16)
        for h in range(HEADS):
            cols = slice(h * HEAD, (h + 1) * HEAD)
            values[u, :, cols] = values[u, :, cols] * keep
        return carry

    lax.fori_loop(0, users, mask_user, 0)

    def early(chunks):
        @pl.when(y < 2)
        def _():
            take(0, chunks)

        @pl.when(y >= 2)
        def _():
            take(1, chunks)

    def early_rest(chunks):
        @pl.when(y < 2)
        def _():
            take(2, chunks)
            take_sibling(3, chunks)
            take_sibling(5, chunks)

        @pl.when(y >= 2)
        def _():
            take_sibling(4, chunks)

    early([0, 1])
    ag_1()
    early([2, 3])
    ag_2()
    ag_3()
    early([4, 5])
    early_rest([0, 1, 2, 3])

    def late_1():
        @pl.when(y < 2)
        def _():
            start_own(1, in_chunks)

        @pl.when(y >= 2)
        def _():
            take(0, in_chunks)

        start_own(0, out_chunks)
        start_own(1, out_chunks)

    def late_2():
        @pl.when(y < 2)
        def _():
            take(1, in_chunks)

        @pl.when(y >= 2)
        def _():
            take(2, in_chunks)

    def late_3():
        take(1, out_chunks)
        take(0, out_chunks)

    def late_4():
        take(2, out_chunks)
        for which in (3, 4, 5):
            take_sibling(which, out_chunks)

        @pl.when(y < 2)
        def _():
            take_sibling(4, in_chunks)

        @pl.when(y >= 2)
        def _():
            take_sibling(3, in_chunks)
            take_sibling(5, in_chunks)

    def make_gate():
        own = normed[own_slot]
        for shard in (0, 1):
            got = jnp.dot(own, w_in[shard], preferred_element_type=jnp.float32)
            gate[:, shard * 512 : (shard + 1) * 512] = silu_of(got, 0.5).astype(jnp.bfloat16)

    def rs_half(a, idx):
        return 1 - a if idx > 0 else a

    def rs_source(g, a, idx, e):
        half = rs_half(a, idx)
        if idx > 0:
            t = place_of(a, e, idx - 1)
            rows = pl.ds(half * HALF, HALF)
            return send.at[g, t, rows, :], part.at[g, t, rows, :]
        return line_send.at[g, half, e], line.at[g, half, e]

    def rs(g, a, dirn, idx, kind):
        e = 2 if kind == 0 else (1 if dirn > 0 else 3)
        first = 0 if (kind != 1) == (dirn > 0) else QUARTER
        w = g * 20 + (a * 2 + (dirn + 1) // 2) * 5 + idx
        src = rs_source(g, a, idx, e)[0].at[pl.ds(first, QUARTER), :]
        dst = far.at[w] if kind == 0 else near.at[w, pl.ds(first, QUARTER), :]
        return remote(
            src, dst, rs_send.at[w * 3 + kind], rs_recv.at[w * 3 + kind], {"seq": neighbour[a, dirn]}
        )

    def rs_any(ref, i, device):
        return remote(ref, ref, rs_send.at[i], rs_recv.at[i], device)

    def rs_first_sends(g, a, idx, e):
        if e == 2:
            rs(g, a, 1, idx, 0).start()
            rs(g, a, -1, idx, 0).start()
        elif e != 0:
            rs(g, a, 1 if e == 1 else -1, idx, 1).start()

    def partial_copy(g, t):
        i = g * UNITS + t
        return remote(part_sib.at[g, t], sib.at[g, t], p_send.at[i], p_recv.at[i], sibling)

    def add_sibling(g, t):
        partial_copy(g, t).wait_recv()
        total = part[g, t] + sib[g, t].astype(jnp.float32)
        part[g, t] = total
        send[g, t] = total.astype(jnp.bfloat16)

    def do_sum(g, t):
        dx, dz = ORDER[t]
        rs_first_sends(g, 1, 1 + dx, dz)
        rs_first_sends(g, 0, 1 + dz, dx)

    def do_dep(g, a, dirn, idx):
        rs(g, a, dirn, idx, 0).wait_recv()
        e, first = (1, 0) if dirn > 0 else (3, QUARTER)
        w = g * 20 + (a * 2 + (dirn + 1) // 2) * 5 + idx
        to_send, exact = rs_source(g, a, idx, e)
        rows = pl.ds(first, QUARTER)
        to_send[rows, :] = (exact[rows, :] + far[w].astype(jnp.float32)).astype(jnp.bfloat16)
        rs(g, a, dirn, idx, 2).start()

    def do_fin(g, a, idx):
        for dirn in (1, -1):
            for kind in (1, 2):
                rs(g, a, dirn, idx, kind).wait_recv()
        up, down = g * 20 + a * 10 + 5 + idx, g * 20 + a * 10 + idx
        exact = rs_source(g, a, idx, 0)[1]
        half = rs_half(a, idx)
        total = exact[...] + near[up].astype(jnp.float32) + near[down].astype(jnp.float32)
        if idx == 0:
            att[half * HALF : (half + 1) * HALF, :] = total
        else:
            line[g, half, idx - 1] = total
            line_send[g, half, idx - 1] = total.astype(jnp.bfloat16)
            rs_first_sends(g, 1 - a, 0, idx - 1)

    steps = {}
    for step, _, g, kind, args in schedule():
        steps.setdefault(step, []).append((kind, (g,) + args))

    def run_step(step):
        for kind, args in steps.get(step, []):
            {"sum": do_sum, "dep": do_dep, "fin": do_fin}[kind](*args)

    def queries_copy(i, shard, batch, group):
        rows = pl.ds(pl.multiple_of(batch * 4 * ROWS, ROWS), 4 * ROWS)
        cols = pl.ds(pl.multiple_of(shard * 512 + group * 256, 256), 256)
        j = i * 2 + shard
        return remote(q_own.at[rows, cols], q_sib.at[rows, cols], q_sems.at[j], q_sems.at[16 + j], sibling)

    def project(i, batch, group):
        code_x, code_z = digits(CODES_X, batch), digits(CODES_Z, batch)
        for m in range(4):
            dx, dz = lax.rem(lax.div(code_x, 4**m), 4), lax.rem(lax.div(code_z, 4**m), 4)
            slot = lax.rem(x + dx, 4) * 4 + lax.rem(z + dz, 4)
            stage[m * ROWS : (m + 1) * ROWS, :] = normed[slot]
        rows = pl.ds(pl.multiple_of(batch * 4 * ROWS, ROWS), 4 * ROWS)
        got = [
            jnp.dot(
                stage[...], w_in[2 + shard, :, pl.ds(pl.multiple_of(group * 256, 256), 256)],
                preferred_element_type=jnp.float32,
            )
            for shard in range(2)
        ]
        for shard in range(2):
            cols = pl.ds(pl.multiple_of(shard * 512 + group * 256, 256), 256)
            q_own[rows, cols] = silu_of(got[shard], 0.5).astype(jnp.bfloat16)
            queries_copy(i, shard, batch, group).start()

    half_scale = 0.5 / math.sqrt(HEAD)

    def unit(t, group, code_x, code_z):
        blocks = []
        for n in range(2):
            dx, dz = lax.rem(lax.div(code_x, 4**n), 4), lax.rem(lax.div(code_z, 4**n), 4)
            chip = lax.rem(x + dx, 4) * 4 + lax.rem(z + dz, 4)
            rows = pl.ds(pl.multiple_of((t + n) * ROWS, ROWS), ROWS)
            blocks.append((0, t + n, rows, owner_ref[2 * chip + core]))
            blocks.append((1, t + n, rows, owner_ref[2 * chip + 1 - core]))
        starts = [shard * 512 + group * 256 + h * HEAD for shard in range(2) for h in range(2)]
        heads = [slice(start, start + HEAD) for start in starts]
        items = [(block, i) for block in blocks for i in range(len(heads))]

        def scores_of(i):
            (sibs, _, rows, owner), cols = items[i][0], heads[items[i][1]]
            return lax.dot_general(
                keys[owner, :, cols], (q_own, q_sib)[sibs][rows, cols],
                (((1,), (1,)), ((), ())), preferred_element_type=jnp.float32,
            )

        pending = [scores_of(0), scores_of(1)]
        for i, ((sibs, at, rows, owner), n) in enumerate(items):
            cols = heads[n]
            if i + 2 < len(items):
                pending.append(scores_of(i + 2))
            weights = silu_of(pending.pop(0), half_scale).astype(jnp.bfloat16)
            got = lax.dot_general(
                weights, values[owner, :, cols],
                (((0,), (0,)), ((), ())), preferred_element_type=jnp.float32,
            )
            if sibs == 0:
                part[0, at, :, cols] = got
            else:
                part_sib[0, at, :, cols] = got.astype(jnp.bfloat16)

    def early_3():
        early([6, 7])

    extras = {
        0: [early_3, ag_4], 1: [ag_5], 2: [ag_6, late_1], 4: [ag_7],
        12: [late_2], 14: [late_3],
    }

    def step_body(s, carry):
        to_project, to_attend, to_add = carry

        @pl.when(s == 4)
        def _():
            early_rest([4, 5, 6, 7])

        @pl.when((lax.rem(s, 2) == 0) & (s < STEPS))
        def _():
            project(lax.div(s, 2), lax.rem(to_project, 4), lax.rem(lax.div(to_project, 4), 2))

        @pl.when((s >= 1) & (s <= STEPS))
        def _():
            it = s - 1
            batch, group = lax.rem(to_attend, 4), lax.rem(lax.div(to_attend, 4), 2)
            second = lax.rem(it, 2)
            t = batch * 4 + second * 2

            @pl.when(second == 0)
            def _():
                for shard in range(2):
                    queries_copy(lax.div(it, 2), shard, batch, group).wait_recv()

            code_x = shifted(digits(CODES_X, batch), 16, second)
            code_z = shifted(digits(CODES_Z, batch), 16, second)
            for g in range(2):

                @pl.when(group == g)
                def _(g=g):
                    unit(t, g, code_x, code_z)

            @pl.when(group == 1)
            def _():
                partial_copy(0, t).start()
                partial_copy(0, t + 1).start()

        @pl.when((s >= 2) & (lax.rem(lax.div(to_add, 4), 2) == 1))
        def _():
            t = lax.rem(to_add, 4) * 4 + lax.rem(s, 2) * 2
            add_sibling(0, t)
            add_sibling(0, t + 1)

        for k in range(STEPS + 2):
            todo = extras.get(k, [])
            if todo or k in steps:

                @pl.when(s == k)
                def _(k=k, todo=todo):
                    for action in todo:
                        action()
                    run_step(k)

        odd, late_enough, later = lax.rem(s, 2), lax.div(s + 15, 16), lax.div(s + 13, 16)
        return (
            shifted(to_project, 8, odd),
            shifted(to_attend, 8, (1 - odd) * late_enough),
            shifted(to_add, 8, odd * later),
        )

    lax.fori_loop(0, STEPS + 2, step_body, (CODE, CODE, CODE))
    late = [step for step in sorted(steps) if step > STEPS + 1]
    def sent(count, copy_of):
        for i in range(count):
            copy_of(i).wait_send()

    east = {"seq": neighbour[0, 1]}
    for rows, first in ((HALF, 0), (QUARTER, 1)):
        block = normed.at[0, pl.ds(0, rows), :]
        sent(20, lambda i, block=block, first=first: ag_any(block, 2 * i + first, east))
    for shard in range(2):
        sent(8, lambda i, shard=shard: queries_copy(i, shard, 0, 0))
    run_step(late[0])
    late_4()
    make_gate()
    for which in range(6):
        sent(CHUNKS, lambda chunk, which=which: weight(which, chunk))
        weight(which, CHUNKS).wait_send()
    for step in late[1:]:
        run_step(step)

    def norm_att(rows):
        gated = normalize(att[rows, :]) * gate[rows, :].astype(jnp.float32)
        gate[rows, :] = gated.astype(jnp.bfloat16)

    by_rows(ROWS, norm_att)

    branch = jnp.dot(
        gate[...], w_out[...].reshape(WIDTH, WIDTH), preferred_element_type=jnp.float32
    )
    out_ref[...] = (cand_ref[...].astype(jnp.float32) + branch).astype(jnp.bfloat16)

    sent(60, lambda i: rs_any(far.at[0], i, east))
    sent(UNITS, lambda t: partial_copy(0, t))


def per_device(candidates, block_user, hist_len, key_cache, value_cache, w_in, w_out):
    users, span, width = key_cache.shape[1:]
    vmem = pl.BlockSpec(memory_space=pltpu.VMEM)
    smem = pl.BlockSpec(memory_space=pltpu.SMEM)
    anywhere = pl.BlockSpec(memory_space=pl.ANY)
    bf16, f32 = jnp.bfloat16, jnp.float32
    dma = pltpu.SemaphoreType.DMA
    updated = pl.pallas_call(
        layer_kernel,
        out_shape=jax.ShapeDtypeStruct((ROWS, width), bf16),
        in_specs=[smem, smem, vmem, anywhere, anywhere, anywhere, anywhere],
        out_specs=vmem,
        scratch_shapes=[
            pltpu.VMEM((users, span, width), bf16),
            pltpu.VMEM((users, span, width), bf16),
            pltpu.VMEM((4,) + w_in.shape, bf16),
            pltpu.VMEM((4,) + w_out.shape, bf16),
            pltpu.VMEM((UNITS, ROWS, width), bf16),
            pltpu.VMEM((4 * ROWS, width), bf16),
            pltpu.VMEM((UNITS * ROWS, width), bf16),
            pltpu.VMEM((UNITS * ROWS, width), bf16),
            pltpu.VMEM((1, UNITS, ROWS, width), f32),
            pltpu.VMEM((1, UNITS, ROWS, width), bf16),
            pltpu.VMEM((1, UNITS, ROWS, width), bf16),
            pltpu.VMEM((1, UNITS, ROWS, width), bf16),
            pltpu.VMEM((20, QUARTER, width), bf16),
            pltpu.VMEM((20, HALF, width), bf16),
            pltpu.VMEM((1, 2, 4, HALF, width), f32),
            pltpu.VMEM((1, 2, 4, HALF, width), bf16),
            pltpu.VMEM((ROWS, width), f32),
            pltpu.VMEM((ROWS, width), bf16),
            dma((4,)),
            dma((40,)),
            dma((40,)),
            dma((6 * (CHUNKS + 1),)),
            dma((6 * (CHUNKS + 1),)),
            dma((32,)),
            dma((UNITS,)),
            dma((UNITS,)),
            dma((60,)),
            dma((60,)),
        ],
        compiler_params=pltpu.CompilerParams(
            collective_id=0, has_side_effects=True, vmem_limit_bytes=60 << 20
        ),
        name="layer",
    )(
        block_user[0], hist_len[0], candidates[0, 0], key_cache[0], value_cache[0], w_in, w_out
    )
    return updated.reshape(candidates.shape)


def solution(mesh):
    in_specs = (
        P("grp", "seq", None, None),
        P("grp", None),
        P("grp", None),
        P("grp", None, "seq", None),
        P("grp", None, "seq", None),
        P(None, "grp"),
        P("grp", None),
    )
    out_specs = P("grp", "seq", None, None)
    return jax.shard_map(
        per_device, mesh=mesh, in_specs=in_specs, out_specs=out_specs, check_vma=False
    )
```
